128 devices in a mesh: row: 8 (over y, core), col: 16 (over z, x).
Axes of the slice: x: 4, y: 4, z: 4, core: 2. Of those that a mesh axis runs over, the one named last changes fastest.
Arguments:
- weight: bfloat16 [8192, 26624], P('row', 'col'), may hold values from -6 to 6
- momentum: float32 [8192, 26624], P('row', 'col'), may hold values from -6 to 6
- gradient: bfloat16 [8192, 26624], P('row', 'col'), may hold values from -6 to 6
- right_factor: float32 [26624, 128], P('col'), may hold values from -6 to 6
Outputs:
- new_weight: bfloat16 [8192, 26624], P('row', 'col')
- new_momentum: float32 [8192, 26624], P('row', 'col')
- new_right: float32 [26624, 128], P('col')
The draws below stay inside these ranges and needn't reach their ends.
All inputs are finite; a program needn't handle non-finite values.
Results may differ from the reference program's by a relative error of at most 0.001.
Values sent between devices are 32-bit elements; how exact they have to be, the bound alone decides.
A program may use at most 128 MiB of HBM per device.

```python
import jax
import jax.numpy as jnp
from jax import lax

ROWS = 8192
COLS = 26624
RANK = 128


def steps_of(stream_key, shape, pieces, least, high):
    level = 1.0
    for position, blocks in pieces:
        steps = jax.random.uniform(jax.random.fold_in(jax.random.fold_in(stream_key, 6), position), (blocks,), jnp.float32, least / len(pieces), high / len(pieces))
        level = level * jnp.repeat(jnp.exp(steps), shape[position] // blocks).reshape((-1,) + (1,) * (len(shape) - 1 - position))
    return level


def centred(own_key, extent, spread, reach, pieces=(), held_as=jnp.bfloat16):
    gain = steps_of(own_key, extent, pieces, -0.22, 0.18) if pieces else 1.0
    entries = jax.random.normal(own_key, extent, jnp.float32) * spread * gain
    return jnp.minimum(jnp.maximum(entries, -reach), reach).astype(held_as)


def setup_inputs(seed: int = 0) -> dict:
    key_list = jax.random.split(jax.random.key(seed), 5)
    weight = centred(key_list[0], (ROWS, COLS), 1.0, 6.0, ((0, 8), (1, 16)))
    momentum = centred(key_list[1], (ROWS, COLS), 1.0, 6.0, ((0, 8), (1, 16)), jnp.float32)
    gradient = centred(key_list[2], (ROWS, COLS), 1.0, 6.0, ((0, 8), (1, 16)))
    right_factor = centred(key_list[3], (COLS, RANK), 1.0, 6.0, ((0, 16),), jnp.float32)
    return {"weight": weight, "momentum": momentum, "gradient": gradient, "right_factor": right_factor}


def reference(weight, momentum, gradient, right_factor):
    hi = lax.Precision.HIGHEST
    accum = momentum + gradient.astype(jnp.float32)
    panel = jnp.dot(accum, right_factor, precision=hi)
    gram = jnp.dot(panel.T, panel, precision=hi)
    lower = jnp.linalg.cholesky(gram)
    ortho = lax.linalg.triangular_solve(lower, panel, left_side=False, lower=True, transpose_a=True)
    right = jnp.dot(accum.T, ortho, precision=hi)
    new_momentum = accum - 0.2 * jnp.dot(ortho, right.T, precision=hi)
    norms = jnp.sqrt(lax.optimization_barrier(jnp.sum(right * right, axis=0)) + 1e-06)
    new_right = right * (jnp.sqrt(jnp.float32(COLS)) / norms)
    factor = 0.5 * jnp.sqrt(jnp.float32(ROWS) / jnp.float32(RANK))
    new_weight = (weight.astype(jnp.float32) - factor * jnp.dot(ortho, new_right.T, precision=hi)).astype(jnp.bfloat16)
    return (new_weight, new_momentum, new_right)
```

```python
import functools

import jax
import jax.numpy as jnp
from jax import lax
from jax.experimental import pallas as pl
from jax.experimental.pallas import tpu as pltpu
from jax.sharding import PartitionSpec as P

ROWS = 8192
COLS = 26624
RANK = 128
HI = lax.Precision.HIGHEST
MESH = pl.DeviceIdType.MESH
F32 = jnp.float32
BF16 = jnp.bfloat16

ZS, XS, YS, CORES = 4, 4, 4, 2
COL_DEVS = ZS * XS
ROW_DEVS = YS * CORES
MY_ROWS = ROWS // ROW_DEVS
MY_COLS = COLS // COL_DEVS
OWN = MY_ROWS // COL_DEVS
GROUP = OWN * XS
GROUPS = MY_ROWS // GROUP
GRAM_OWN = RANK // ROW_DEVS
HALF = RANK // CORES
BLOCK = HALF // YS
SUB = BLOCK // 2
CHUNKS = ((0, 896), (896, 768))
NCH = len(CHUNKS)
PIVOTS = 16

CORE, UP_RELAY, UP_OWN, DOWN_RELAY, DOWN_OWN, UP_SUM, DOWN_SUM = range(7)
AG_UP, AG_DOWN, AG_UP_HALF, AG_DOWN_HALF, PAIR_OWN, PAIR_UP, PAIR_DOWN, PAIR_UP_HALF, PAIR_DOWN_HALF = range(7, 16)
KINDS = 16


def dot(a, b, precision=None):
    return jnp.dot(a, b, precision=precision, preferred_element_type=F32)


def iota(shape, dim):
    return lax.broadcasted_iota(jnp.int32, shape, dim)


def eliminate(rows, first):
    ri, ci = iota(rows.shape, 0), iota(rows.shape, 1)
    cols = [jnp.broadcast_to(rows[:, first + j : first + j + 1], rows.shape) for j in range(PIVOTS)]
    for k in range(PIVOTS):
        scale = lax.rsqrt(cols[k][k : k + 1, :])
        row = jnp.where(ci[:1] == first + k, scale, rows[k : k + 1, :] * scale)
        mult = jnp.where(ri > k, cols[k] * scale, 0.0)
        cleared = jnp.where((ci == first + k) & (ri > k), 0.0, rows)
        rows = jnp.where(ri == k, row, cleared - mult * row)
        for j in range(k + 1, PIVOTS):
            cols[j] = cols[j] - mult * (cols[j][k : k + 1, :] * scale)
    return jnp.where((ci > ri + first) & (ci < first + PIVOTS), 0.0, rows)


def cholesky_block(work, block):
    first = block * PIVOTS
    after = first + PIVOTS
    done = eliminate(work[first:after, :], first)
    work[first:after, :] = done
    if after < RANK:
        ci = iota(done.shape, 1)
        factor = jnp.where(ci >= after, done, 0.0).T
        rest = work[after:, :]
        cj = iota(rest.shape, 1)
        rest = jnp.where((cj >= first) & (cj < after), 0.0, rest)
        work[after:, :] = rest - dot(factor[after:, :], done, HI)


def main_kernel(
    mom, grad, rf, w,
    nm, wv, ortho, rt, sq,
    hi, lo, gbuf, rbuf, rcat, psend, prs, pan, pt, gram_part, gram_in, gram, sloc, cbuf, ys, yin, stf, sq_send, sq_in,
    load_sem, mom_sem, grad_sem,
    rs_send, rs_recv, ag_send, ag_recv, gs_send, gs_recv, ga_send, ga_recv, y_send, y_recv, q_send, q_recv,
):
    row = lax.axis_index("row")
    col = lax.axis_index("col")
    y, core = row // CORES, row % CORES
    z, x = col // XS, col % XS
    pair = (y * CORES + 1 - core, col)
    up = (((y + 1) % YS) * CORES + core, col)
    down = (((y + YS - 1) % YS) * CORES + core, col)

    rf_copy = pltpu.make_async_copy(rf, rbuf, load_sem.at[0])
    rf_copy.start()
    g0 = (x + z) % GROUPS

    def group_of(j):
        return (g0 + 1 + j) % GROUPS

    def load(j):
        rows = pl.ds(pl.multiple_of(group_of(j) * GROUP, GROUP), GROUP)
        return (
            pltpu.make_async_copy(mom.at[rows, :], nm.at[rows, :], mom_sem.at[j]),
            pltpu.make_async_copy(grad.at[rows, :], gbuf.at[rows, :], grad_sem.at[j]),
        )

    for j in range(GROUPS):
        for c in load(j):
            c.start()
    w_copy = pltpu.make_async_copy(w, wv, load_sem.at[1])
    w_copy.start()

    barrier = pltpu.get_barrier_semaphore()

    def greet_col(k, _):
        pl.semaphore_signal(barrier, inc=1, device_id=(row, (col + k) % COL_DEVS), device_id_type=MESH)
        return 0

    def greet_row(k, _):
        pl.semaphore_signal(barrier, inc=1, device_id=((row + k) % ROW_DEVS, col), device_id_type=MESH)
        return 0

    lax.fori_loop(1, COL_DEVS, greet_col, 0)
    lax.fori_loop(1, ROW_DEVS, greet_row, 0)

    rf_copy.wait()
    r = rbuf[...]
    rh = r.astype(BF16)
    rcat[:, :RANK] = rh
    rcat[:, RANK:] = (r - rh.astype(F32)).astype(BF16)
    pl.semaphore_wait(barrier, COL_DEVS - 1 + ROW_DEVS - 1)

    def own_rows(c):
        cz, cx = c // XS, c % XS
        return pl.ds(pl.multiple_of((((cx + cz) % GROUPS) * XS + cx) * OWN, OWN), OWN)

    def rs_copy(to, slot):
        return pltpu.make_async_remote_copy(
            src_ref=psend.at[own_rows(to), :], dst_ref=prs.at[slot], send_sem=rs_send.at[to], recv_sem=rs_recv.at[slot],
            device_id=(row, to), device_id_type=MESH)

    def panel_group(j, _):
        for c in load(j):
            c.wait()
        g = group_of(j)
        base = pl.multiple_of(g * GROUP, GROUP)

        def split(i, _):
            rows = pl.ds(pl.multiple_of(base + i * 32, 32), 32)
            a = nm[rows, :] + gbuf[rows, :].astype(F32)
            nm[rows, :] = a
            h = a.astype(BF16)
            hi[rows, :] = h
            lo[rows, :] = (a - h.astype(F32)).astype(BF16)
            return 0

        lax.fori_loop(0, GROUP // 32, split, 0)
        rows = pl.ds(base, GROUP)
        p = dot(hi[rows, :], rcat[...])
        psend[rows, :] = p[:, :RANK] + p[:, RANK:] + dot(lo[rows, :], rcat[:, :RANK])
        for t in range(XS):
            to = ((g + GROUPS - t) % GROUPS) * XS + t

            @pl.when(to != col)
            def _():
                rs_copy(to, col).start()

        return 0

    lax.fori_loop(0, GROUPS, panel_group, 0)

    mine = own_rows(col)

    def rs_sum(k, acc):
        src = (col + k) % COL_DEVS
        rs_copy(src, src).wait_recv()
        return acc + prs[src]

    pan[mine, :] = lax.fori_loop(1, COL_DEVS, rs_sum, psend[mine, :])

    def ag_copy(to, owner):
        rows = own_rows(owner)
        return pltpu.make_async_remote_copy(
            src_ref=pan.at[rows, :], dst_ref=pan.at[rows, :], send_sem=ag_send.at[to], recv_sem=ag_recv.at[owner],
            device_id=(row, to), device_id_type=MESH)

    def ag_start(k, _):
        ag_copy((col + k) % COL_DEVS, col).start()
        return 0

    lax.fori_loop(1, COL_DEVS, ag_start, 0)

    def ag_wait(k, _):
        src = (col + k) % COL_DEVS
        ag_copy(src, src).wait_recv()
        return 0

    lax.fori_loop(1, COL_DEVS, ag_wait, 0)

    p = pan[...]
    p_t = p.T
    ph = p_t.astype(BF16)
    pt[:RANK, :] = ph
    pt[RANK:, :] = (p_t - ph.astype(F32)).astype(BF16)
    gram_part[...] = dot(p_t, p, HI)

    def gram_rows(c):
        return pl.ds(pl.multiple_of(c * GRAM_OWN, GRAM_OWN), GRAM_OWN)

    def gs_copy(to, slot):
        return pltpu.make_async_remote_copy(
            src_ref=gram_part.at[gram_rows(to), :], dst_ref=gram_in.at[slot], send_sem=gs_send.at[to], recv_sem=gs_recv.at[slot],
            device_id=(to, col), device_id_type=MESH)

    def gs_start(k, _):
        gs_copy((row + k) % ROW_DEVS, row).start()
        return 0

    lax.fori_loop(1, ROW_DEVS, gs_start, 0)

    def ycopy(kind, c, src, dst, to):
        return pltpu.make_async_remote_copy(
            src_ref=src, dst_ref=dst, send_sem=y_send.at[c, kind], recv_sem=y_recv.at[c, kind], device_id=to, device_id_type=MESH)

    def lanes(c):
        return pl.ds(CHUNKS[c][0], CHUNKS[c][1])

    def core_copy(c):
        theirs = pl.ds(pl.multiple_of((1 - core) * HALF, HALF), HALF)
        return ycopy(CORE, c, sloc.at[theirs, lanes(c)], cbuf.at[:, lanes(c)], pair)

    for c in range(NCH):
        t = dot(pt[...], hi[:, lanes(c)])
        sloc[:, lanes(c)] = t[:RANK] + t[RANK:] + dot(pt[:RANK, :], lo[:, lanes(c)])
        core_copy(c).start()

    def ga_copy(to, owner):
        return pltpu.make_async_remote_copy(
            src_ref=gram.at[gram_rows(owner), :], dst_ref=gram.at[gram_rows(owner), :], send_sem=ga_send.at[to], recv_sem=ga_recv.at[owner],
            device_id=(to, col), device_id_type=MESH)

    def gs_sum(k, acc):
        src = (row + k) % ROW_DEVS
        gs_copy(src, src).wait_recv()
        return acc + gram_in[src]

    gram[gram_rows(row), :] = lax.fori_loop(1, ROW_DEVS, gs_sum, gram_part[gram_rows(row), :])

    def ga_start(k, _):
        ga_copy((row + k) % ROW_DEVS, row).start()
        return 0

    lax.fori_loop(1, ROW_DEVS, ga_start, 0)

    def block(ref, b, half, c):
        start = pl.multiple_of((b % YS) * BLOCK + half * SUB, SUB)
        return ref.at[pl.ds(start, SUB), lanes(c)]

    TOP, BOTTOM = 0, 1

    def relay_copies(c):
        return (
            ycopy(UP_RELAY, c, block(ys, y + 2, TOP, c), yin.at[UP_RELAY, :, lanes(c)], up),
            ycopy(DOWN_RELAY, c, block(ys, y + 2, BOTTOM, c), yin.at[DOWN_RELAY, :, lanes(c)], down),
            ycopy(UP_OWN, c, block(ys, y + 1, BOTTOM, c), yin.at[UP_OWN, :, lanes(c)], up),
            ycopy(DOWN_OWN, c, block(ys, y + 3, TOP, c), yin.at[DOWN_OWN, :, lanes(c)], down),
        )

    def sum_copies(c):
        return (
            ycopy(UP_SUM, c, block(ys, y + 1, TOP, c), yin.at[UP_SUM, :, lanes(c)], up),
            ycopy(DOWN_SUM, c, block(ys, y + 3, BOTTOM, c), yin.at[DOWN_SUM, :, lanes(c)], down),
        )

    def scatter_1(c):
        core_copy(c).wait_recv()
        ours = pl.ds(pl.multiple_of(core * HALF, HALF), HALF)
        ys[:, lanes(c)] = sloc[ours, lanes(c)] + cbuf[:, lanes(c)]
        for cp in relay_copies(c):
            cp.start()

    def scatter_2(c):
        relays = relay_copies(c)
        sums = sum_copies(c)
        for relay, total, kind in ((relays[0], sums[0], UP_RELAY), (relays[1], sums[1], DOWN_RELAY)):
            relay.wait_recv()
            start = (y + 1) % YS * BLOCK if kind == UP_RELAY else (y + 3) % YS * BLOCK + SUB
            rows = pl.ds(pl.multiple_of(start, SUB), SUB)
            ys[rows, lanes(c)] = ys[rows, lanes(c)] + yin[kind, :, lanes(c)]
            total.start()

    def st_block(b, half, c):
        start = pl.multiple_of(core * HALF + (b % YS) * BLOCK + (half or 0) * SUB, SUB)
        return stf.at[pl.ds(start, BLOCK if half is None else SUB), lanes(c)]

    def gather_copies(c):
        own, above, below = st_block(y, None, c), st_block(y + 1, None, c), st_block(y + 3, None, c)
        far_top, far_bottom = st_block(y + 2, TOP, c), st_block(y + 2, BOTTOM, c)
        up_half, down_half = st_block(y + 3, TOP, c), st_block(y + 1, BOTTOM, c)
        return {
            AG_UP: ycopy(AG_UP, c, own, own, up),
            AG_DOWN: ycopy(AG_DOWN, c, own, own, down),
            PAIR_OWN: ycopy(PAIR_OWN, c, own, own, pair),
            AG_UP_HALF: ycopy(AG_UP_HALF, c, up_half, up_half, up),
            AG_DOWN_HALF: ycopy(AG_DOWN_HALF, c, down_half, down_half, down),
            PAIR_UP: ycopy(PAIR_UP, c, below, below, pair),
            PAIR_DOWN: ycopy(PAIR_DOWN, c, above, above, pair),
            PAIR_UP_HALF: ycopy(PAIR_UP_HALF, c, far_top, far_top, pair),
            PAIR_DOWN_HALF: ycopy(PAIR_DOWN_HALF, c, far_bottom, far_bottom, pair),
        }

    def gather_1(c):
        relays = relay_copies(c)
        sums = sum_copies(c)
        for cp in (relays[2], relays[3], sums[0], sums[1]):
            cp.wait_recv()
        top = pl.ds(pl.multiple_of(y * BLOCK, SUB), SUB)
        bottom = pl.ds(pl.multiple_of(y * BLOCK + SUB, SUB), SUB)
        at_top = pl.ds(pl.multiple_of(core * HALF + y * BLOCK, SUB), SUB)
        at_bottom = pl.ds(pl.multiple_of(core * HALF + y * BLOCK + SUB, SUB), SUB)
        stf[at_top, lanes(c)] = ys[top, lanes(c)] + yin[UP_SUM, :, lanes(c)] + yin[DOWN_OWN, :, lanes(c)]
        stf[at_bottom, lanes(c)] = ys[bottom, lanes(c)] + yin[DOWN_SUM, :, lanes(c)] + yin[UP_OWN, :, lanes(c)]
        cps = gather_copies(c)
        for kind in (AG_UP, AG_DOWN, PAIR_OWN):
            cps[kind].start()

    def gather_2(c):
        cps = gather_copies(c)
        for got, onward in ((AG_UP, (AG_UP_HALF, PAIR_UP)), (AG_DOWN, (AG_DOWN_HALF, PAIR_DOWN))):
            cps[got].wait_recv()
            for kind in onward:
                cps[kind].start()

    def gather_3(c):
        cps = gather_copies(c)
        for got, onward in ((AG_UP_HALF, PAIR_UP_HALF), (AG_DOWN_HALF, PAIR_DOWN_HALF)):
            cps[got].wait_recv()
            cps[onward].start()

    def gather_4(c):
        cps = gather_copies(c)
        for kind in (PAIR_OWN, PAIR_UP, PAIR_DOWN, PAIR_UP_HALF, PAIR_DOWN_HALF):
            cps[kind].wait_recv()

    scatter_1(0)
    scatter_1(1)

    def ga_wait(k, _):
        src = (row + k) % ROW_DEVS
        ga_copy(src, src).wait_recv()
        return 0

    lax.fori_loop(1, ROW_DEVS, ga_wait, 0)

    def ga_sent(k, _):
        ga_copy((row + k) % ROW_DEVS, row).wait_send()
        gs_copy((row + k) % ROW_DEVS, row).wait_send()
        return 0

    lax.fori_loop(1, ROW_DEVS, ga_sent, 0)

    steps = {
        0: lambda: scatter_2(0),
        1: lambda: scatter_2(1),
        2: lambda: gather_1(0),
        3: lambda: gather_1(1),
        4: lambda: gather_2(0),
        5: lambda: gather_2(1),
        6: lambda: gather_3(0),
        7: lambda: gather_3(1),
    }
    for b in range(RANK // PIVOTS):
        cholesky_block(gram, b)
        steps[b]()
    inverse = jnp.where(iota((RANK, RANK), 0) >= iota((RANK, RANK), 1), gram[...], 0.0)
    o = lax.dot_general(pan[...], inverse, (((1,), (1,)), ((), ())), precision=HI, preferred_element_type=F32)
    ortho[...] = o

    squares = jnp.zeros((RANK, RANK), F32)
    for c in range(NCH):
        gather_4(c)
        part = dot(inverse, stf[:, lanes(c)], HI)
        rt[:, lanes(c)] = part
        for i in range(CHUNKS[c][1] // RANK):
            tile = part[:, i * RANK : (i + 1) * RANK]
            squares += tile * tile
    sq_send[...] = jnp.broadcast_to(jnp.sum(squares.T, axis=0, keepdims=True), sq_send.shape)

    def q_copy(to, slot):
        return pltpu.make_async_remote_copy(
            src_ref=sq_send, dst_ref=sq_in.at[slot], send_sem=q_send.at[to], recv_sem=q_recv.at[slot],
            device_id=(row, to), device_id_type=MESH)

    def q_start(k, _):
        q_copy((col + k) % COL_DEVS, col).start()
        return 0

    lax.fori_loop(1, COL_DEVS, q_start, 0)

    def momentum(i, _):
        rows = pl.ds(pl.multiple_of(i * 128, 128), 128)
        nm[rows, :] = nm[rows, :] - 0.2 * dot(ortho[rows, :].astype(BF16), rt[...].astype(BF16))
        return 0

    lax.fori_loop(0, MY_ROWS // 128, momentum, 0)

    def q_sum(k, acc):
        src = (col + k) % COL_DEVS
        q_copy(src, src).wait_recv()
        return acc + sq_in[src]

    sq[...] = lax.fori_loop(1, COL_DEVS, q_sum, sq_send[...])

    w_copy.wait()

    def sent(k, _):
        to = (col + k) % COL_DEVS
        rs_copy(to, col).wait_send()
        ag_copy(to, col).wait_send()
        q_copy(to, col).wait_send()
        return 0

    lax.fori_loop(1, COL_DEVS, sent, 0)
    for c in range(NCH):
        for cp in (core_copy(c),) + relay_copies(c) + sum_copies(c) + tuple(gather_copies(c).values()):
            cp.wait_send()


def final_kernel(nm, wv, ortho, rt, sq, new_w, new_m, new_r, out, r_out, oc, rc, m_sem, w_sem, r_sem):
    steps = 8
    size = MY_ROWS // steps
    m_copy = pltpu.make_async_copy(nm, new_m, m_sem)
    m_copy.start()
    scale = jnp.sqrt(F32(COLS)) / jnp.sqrt(sq[:1, :] + 1e-06)
    factor = 0.5 * jnp.sqrt(F32(ROWS) / F32(RANK))
    rh = rt[...].astype(BF16)
    rc[:RANK, :] = rh
    rc[RANK:, :] = (rt[...] - rh.astype(F32)).astype(BF16)
    o = ortho[...] * (scale * factor)
    oh = o.astype(BF16)
    oc[:, :RANK] = oh
    oc[:, RANK:] = (o - oh.astype(F32)).astype(BF16)

    def w_copy(i):
        rows = pl.ds(pl.multiple_of(i * size, size), size)
        return pltpu.make_async_copy(out.at[rows, :], new_w.at[rows, :], w_sem.at[i])

    def weight(i, _):
        rows = pl.ds(pl.multiple_of(i * size, size), size)
        high = oc[rows, :RANK]
        step = dot(high, rc[:RANK, :]) + dot(high, rc[RANK:, :]) + dot(oc[rows, RANK:], rc[:RANK, :])
        out[rows, :] = (wv[rows, :].astype(F32) - step).astype(BF16)
        w_copy(i).start()
        return 0

    lax.fori_loop(0, steps, weight, 0)
    r_out[...] = rt[...].T * scale
    r_copy = pltpu.make_async_copy(r_out, new_r, r_sem)
    r_copy.start()

    def done(i, _):
        w_copy(i).wait()
        return 0

    lax.fori_loop(0, steps, done, 0)
    m_copy.wait()
    r_copy.wait()


def shards(weight, momentum, gradient, right_factor):
    hbm = pl.BlockSpec(memory_space=pltpu.HBM)
    vmem = pl.BlockSpec(memory_space=pltpu.VMEM)
    dma = pltpu.SemaphoreType.DMA
    held = pl.pallas_call(
        main_kernel,
        out_shape=(
            pltpu.VMEM((MY_ROWS, MY_COLS), F32),
            pltpu.VMEM((MY_ROWS, MY_COLS), BF16),
            pltpu.VMEM((MY_ROWS, RANK), F32),
            pltpu.VMEM((RANK, MY_COLS), F32),
            pltpu.VMEM((8, RANK), F32),
        ),
        in_specs=[hbm] * 4,
        out_specs=(vmem,) * 5,
        scratch_shapes=[
            pltpu.VMEM((MY_ROWS, MY_COLS), BF16),
            pltpu.VMEM((MY_ROWS, MY_COLS), BF16),
            pltpu.VMEM((MY_ROWS, MY_COLS), BF16),
            pltpu.VMEM((MY_COLS, RANK), F32),
            pltpu.VMEM((MY_COLS, 2 * RANK), BF16),
            pltpu.VMEM((MY_ROWS, RANK), F32),
            pltpu.VMEM((COL_DEVS, OWN, RANK), F32),
            pltpu.VMEM((MY_ROWS, RANK), F32),
            pltpu.VMEM((2 * RANK, MY_ROWS), BF16),
            pltpu.VMEM((RANK, RANK), F32),
            pltpu.VMEM((ROW_DEVS, GRAM_OWN, RANK), F32),
            pltpu.VMEM((RANK, RANK), F32),
            pltpu.VMEM((RANK, MY_COLS), F32),
            pltpu.VMEM((HALF, MY_COLS), F32),
            pltpu.VMEM((HALF, MY_COLS), F32),
            pltpu.VMEM((7, SUB, MY_COLS), F32),
            pltpu.VMEM((RANK, MY_COLS), F32),
            pltpu.VMEM((8, RANK), F32),
            pltpu.VMEM((COL_DEVS, 8, RANK), F32),
            dma((2,)), dma((GROUPS,)), dma((GROUPS,)),
            dma((COL_DEVS,)), dma((COL_DEVS,)), dma((COL_DEVS,)), dma((COL_DEVS,)),
            dma((ROW_DEVS,)), dma((ROW_DEVS,)), dma((ROW_DEVS,)), dma((ROW_DEVS,)),
            dma((NCH, KINDS)), dma((NCH, KINDS)),
            dma((COL_DEVS,)), dma((COL_DEVS,)),
        ],
        compiler_params=pltpu.CompilerParams(collective_id=0, has_side_effects=True, vmem_limit_bytes=40 << 20),
        name="dion_main",
    )(momentum, gradient, right_factor, weight)
    return pl.pallas_call(
        final_kernel,
        out_shape=(
            jax.ShapeDtypeStruct((MY_ROWS, MY_COLS), BF16),
            jax.ShapeDtypeStruct((MY_ROWS, MY_COLS), F32),
            jax.ShapeDtypeStruct((MY_COLS, RANK), F32),
        ),
        in_specs=[vmem] * 5,
        out_specs=(hbm,) * 3,
        scratch_shapes=[
            pltpu.VMEM((MY_ROWS, MY_COLS), BF16),
            pltpu.VMEM((MY_COLS, RANK), F32),
            pltpu.VMEM((MY_ROWS, 2 * RANK), BF16),
            pltpu.VMEM((2 * RANK, MY_COLS), BF16),
            dma, dma((8,)), dma,
        ],
        compiler_params=pltpu.CompilerParams(vmem_limit_bytes=24 << 20),
        name="dion_final",
    )(*held)


def solution(mesh):
    placed = (P("row", "col"), P("row", "col"), P("row", "col"), P("col", None))
    return jax.shard_map(
        shards,
        mesh=mesh,
        in_specs=placed,
        out_specs=(P("row", "col"), P("row", "col"), P("col", None)),
        check_vma=False,
    )
```

```python
import jax
import jax.numpy as jnp
from jax import lax
from jax.experimental import pallas as pl
from jax.experimental.pallas import tpu as pltpu
from jax.sharding import PartitionSpec as P

ROWS = 8192
COLS = 26624
RANK = 128
HI = lax.Precision.HIGHEST
MESH = pl.DeviceIdType.MESH
F32 = jnp.float32
BF16 = jnp.bfloat16

ZS, XS, YS, CORES = 4, 4, 4, 2
COL_DEVS = ZS * XS
ROW_DEVS = YS * CORES
MY_ROWS = ROWS // ROW_DEVS
MY_COLS = COLS // COL_DEVS
OWN = MY_ROWS // COL_DEVS
GROUP = OWN * XS
GROUPS = MY_ROWS // GROUP
GRAM_OWN = RANK // ROW_DEVS
HALF = RANK // CORES
QUARTER = HALF // 2
CHUNKS = ((0, 512), (512, 512), (1024, 384), (1408, 256))
NCH = len(CHUNKS)
PIVOTS = 16

CORE, FIRST_A, FIRST_B, SECOND_A, SECOND_B, PAIR = range(6)
KINDS = 6


def dot(a, b, precision=None):
    return jnp.dot(a, b, precision=precision, preferred_element_type=F32)


def split(a):
    high = a.astype(BF16)
    return high, (a - high.astype(F32)).astype(BF16)


def dot3(a, b):
    ah, al = split(a)
    bh, bl = split(b)
    return dot(ah, bh) + (dot(ah, bl) + dot(al, bh))


def iota(shape, dim):
    return lax.broadcasted_iota(jnp.int32, shape, dim)


def eliminate(rows, first):
    ri, ci = iota(rows.shape, 0), iota(rows.shape, 1)
    cols = [jnp.broadcast_to(rows[:, first + j : first + j + 1], rows.shape) for j in range(PIVOTS)]
    for k in range(PIVOTS):
        scale = lax.rsqrt(cols[k][k : k + 1, :])
        row = jnp.where(ci[:1] == first + k, scale, rows[k : k + 1, :] * scale)
        mult = jnp.where(ri > k, cols[k] * scale, 0.0)
        cleared = jnp.where((ci == first + k) & (ri > k), 0.0, rows)
        rows = jnp.where(ri == k, row, cleared - mult * row)
        for j in range(k + 1, PIVOTS):
            cols[j] = cols[j] - mult * (cols[j][k : k + 1, :] * scale)
    return jnp.where((ci > ri + first) & (ci < first + PIVOTS), 0.0, rows)


def cholesky_block(work, block):
    first = block * PIVOTS
    after = first + PIVOTS
    done = eliminate(work[first:after, :], first)
    work[first:after, :] = done
    if after < RANK:
        ci = iota(done.shape, 1)
        factor = jnp.where(ci >= after, done, 0.0).T
        rest = work[after:, :]
        cj = iota(rest.shape, 1)
        rest = jnp.where((cj >= first) & (cj < after), 0.0, rest)
        work[after:, :] = rest - dot(factor[after:, :], done, HI)


def main_kernel(
    mom, grad, rf, w,
    nm, wv, ortho, rt, rcut, sq,
    hi, lo, gbuf, rbuf, rcat, psend, prs, pan, pt, gram_part, gram_in, gram, sloc, cbuf, y1, in1, y2, in2, stf, sq_send, sq_in,
    load_sem, mom_sem, grad_sem,
    rs_send, rs_recv, ag_send, ag_recv, gs_send, gs_recv, ga_send, ga_recv, y_send, y_recv, q_send, q_recv,
):
    row = lax.axis_index("row")
    col = lax.axis_index("col")
    y, core = row // CORES, row % CORES
    z, x = col // XS, col % XS
    pair = (y * CORES + 1 - core, col)
    near = ((y + 1 - 2 * (y % 2)) * CORES + core, col)
    far = ((YS - 1 - y) * CORES + core, col)

    rf_copy = pltpu.make_async_copy(rf, rbuf, load_sem.at[0])
    rf_copy.start()
    g0 = (x + z) % GROUPS

    def group_of(j):
        return (g0 + 1 + j) % GROUPS

    def load(j):
        rows = pl.ds(pl.multiple_of(group_of(j) * GROUP, GROUP), GROUP)
        return (
            pltpu.make_async_copy(mom.at[rows, :], nm.at[rows, :], mom_sem.at[j]),
            pltpu.make_async_copy(grad.at[rows, :], gbuf.at[rows, :], grad_sem.at[j]),
        )

    for j in range(GROUPS):
        for c in load(j):
            c.start()

    barrier = pltpu.get_barrier_semaphore()

    def greet_col(k, _):
        pl.semaphore_signal(barrier, inc=1, device_id=(row, (col + k) % COL_DEVS), device_id_type=MESH)
        return 0

    def greet_row(k, _):
        pl.semaphore_signal(barrier, inc=1, device_id=((row + k) % ROW_DEVS, col), device_id_type=MESH)
        return 0

    lax.fori_loop(1, COL_DEVS, greet_col, 0)
    lax.fori_loop(1, ROW_DEVS, greet_row, 0)

    rf_copy.wait()
    rh, rl = split(rbuf[...])
    rcat[:, :RANK] = rh
    rcat[:, RANK:] = rl

    def own_rows(c):
        cz, cx = c // XS, c % XS
        return pl.ds(pl.multiple_of((((cx + cz) % GROUPS) * XS + cx) * OWN, OWN), OWN)

    def rs_copy(to, slot):
        return pltpu.make_async_remote_copy(
            src_ref=psend.at[own_rows(to), :], dst_ref=prs.at[slot], send_sem=rs_send.at[to], recv_sem=rs_recv.at[slot],
            device_id=(row, to), device_id_type=MESH)

    def panel_group(j, _):
        for c in load(j):
            c.wait()
        g = group_of(j)
        rows = pl.ds(pl.multiple_of(g * GROUP, GROUP), GROUP)
        a = nm[rows, :] + gbuf[rows, :].astype(F32)
        nm[rows, :] = a
        ah, al = split(a)
        hi[rows, :] = ah
        lo[rows, :] = al
        p = dot(ah, rcat[...])
        psend[rows, :] = p[:, :RANK] + p[:, RANK:] + dot(al, rcat[:, :RANK])

        @pl.when(j == 0)
        def _():
            pl.semaphore_wait(barrier, COL_DEVS - 1 + ROW_DEVS - 1)

        for t in range(XS):
            to = ((g + GROUPS - t) % GROUPS) * XS + t

            @pl.when(to != col)
            def _():
                rs_copy(to, col).start()

        return 0

    lax.fori_loop(0, GROUPS, panel_group, 0)
    w_copy = pltpu.make_async_copy(w, wv, load_sem.at[1])
    w_copy.start()

    mine = own_rows(col)

    def rs_sum(k, acc):
        src = (col + k) % COL_DEVS
        rs_copy(src, src).wait_recv()
        return acc + prs[src]

    pan[mine, :] = lax.fori_loop(1, COL_DEVS, rs_sum, psend[mine, :])

    def ag_copy(to, owner):
        rows = own_rows(owner)
        return pltpu.make_async_remote_copy(
            src_ref=pan.at[rows, :], dst_ref=pan.at[rows, :], send_sem=ag_send.at[to], recv_sem=ag_recv.at[owner],
            device_id=(row, to), device_id_type=MESH)

    def ag_start(k, _):
        ag_copy((col + k) % COL_DEVS, col).start()
        return 0

    lax.fori_loop(1, COL_DEVS, ag_start, 0)

    def ag_wait(k, _):
        src = (col + k) % COL_DEVS
        ag_copy(src, src).wait_recv()
        return 0

    lax.fori_loop(1, COL_DEVS, ag_wait, 0)

    p = pan[...]
    p_t = p.T
    ph, p_low = split(p_t)
    pt[:RANK, :] = ph
    pt[RANK:, :] = p_low
    gram_part[...] = dot(p_t, p, HI)

    def gram_rows(c):
        return pl.ds(pl.multiple_of(c * GRAM_OWN, GRAM_OWN), GRAM_OWN)

    def gs_copy(to, slot):
        return pltpu.make_async_remote_copy(
            src_ref=gram_part.at[gram_rows(to), :], dst_ref=gram_in.at[slot], send_sem=gs_send.at[to], recv_sem=gs_recv.at[slot],
            device_id=(to, col), device_id_type=MESH)

    def gs_start(k, _):
        gs_copy((row + k) % ROW_DEVS, row).start()
        return 0

    lax.fori_loop(1, ROW_DEVS, gs_start, 0)

    def ycopy(kind, c, src, dst, to):
        return pltpu.make_async_remote_copy(
            src_ref=src, dst_ref=dst, send_sem=y_send.at[c, kind], recv_sem=y_recv.at[c, kind], device_id=to, device_id_type=MESH)

    def lanes(c):
        return pl.ds(CHUNKS[c][0], CHUNKS[c][1])

    def core_copy(c):
        theirs = pl.ds(pl.multiple_of((1 - core) * HALF, HALF), HALF)
        return ycopy(CORE, c, sloc.at[theirs, lanes(c)], cbuf.at[:, lanes(c)], pair)

    def quarter(ref, part, c):
        return ref.at[pl.ds(part * QUARTER, QUARTER), lanes(c)]

    def first_copies(c):
        return (
            ycopy(FIRST_A, c, quarter(y1, 0, c), quarter(in1, 0, c), near),
            ycopy(FIRST_B, c, quarter(y1, 1, c), quarter(in1, 1, c), far),
        )

    def second_copies(c):
        return (
            ycopy(SECOND_A, c, quarter(y2, 0, c), quarter(in2, 0, c), far),
            ycopy(SECOND_B, c, quarter(y2, 1, c), quarter(in2, 1, c), near),
        )

    ours = pl.ds(pl.multiple_of(core * HALF, HALF), HALF)

    def pair_copy(c):
        return ycopy(PAIR, c, stf.at[ours, lanes(c)], stf.at[ours, lanes(c)], pair)

    def first(c):
        core_copy(c).wait_recv()
        y1[:, lanes(c)] = sloc[ours, lanes(c)] + cbuf[:, lanes(c)]
        for cp in first_copies(c):
            cp.start()

    def second(c):
        for part, cp in enumerate(first_copies(c)):
            cp.wait_recv()
            at = pl.ds(part * QUARTER, QUARTER)
            y2[at, lanes(c)] = y1[at, lanes(c)] + in1[at, lanes(c)]
            second_copies(c)[part].start()

    def third(c):
        for cp in second_copies(c):
            cp.wait_recv()
        stf[ours, lanes(c)] = y2[:, lanes(c)] + in2[:, lanes(c)]
        pair_copy(c).start()

    for c in range(NCH):
        t = dot(pt[...], hi[:, lanes(c)])
        sloc[:, lanes(c)] = t[:RANK] + t[RANK:] + dot(pt[:RANK, :], lo[:, lanes(c)])
        core_copy(c).start()
        if c:
            first(c - 1)
    first(NCH - 1)

    def ga_copy(to, owner):
        return pltpu.make_async_remote_copy(
            src_ref=gram.at[gram_rows(owner), :], dst_ref=gram.at[gram_rows(owner), :], send_sem=ga_send.at[to], recv_sem=ga_recv.at[owner],
            device_id=(to, col), device_id_type=MESH)

    def gs_sum(k, acc):
        src = (row + k) % ROW_DEVS
        gs_copy(src, src).wait_recv()
        return acc + gram_in[src]

    gram[gram_rows(row), :] = lax.fori_loop(1, ROW_DEVS, gs_sum, gram_part[gram_rows(row), :])

    def ga_start(k, _):
        ga_copy((row + k) % ROW_DEVS, row).start()
        return 0

    lax.fori_loop(1, ROW_DEVS, ga_start, 0)

    for c in range(NCH):
        second(c)

    def ga_wait(k, _):
        src = (row + k) % ROW_DEVS
        ga_copy(src, src).wait_recv()
        return 0

    lax.fori_loop(1, ROW_DEVS, ga_wait, 0)

    def ga_sent(k, _):
        ga_copy((row + k) % ROW_DEVS, row).wait_send()
        gs_copy((row + k) % ROW_DEVS, row).wait_send()
        return 0

    lax.fori_loop(1, ROW_DEVS, ga_sent, 0)

    for b in range(RANK // PIVOTS):
        cholesky_block(gram, b)
        if b % 2 == 1:
            third(b // 2)
    inverse = jnp.where(iota((RANK, RANK), 0) >= iota((RANK, RANK), 1), gram[...], 0.0)
    ortho[...] = dot3(pan[...], inverse.T)

    squares = jnp.zeros((RANK, RANK), F32)
    for c in range(NCH):
        pair_copy(c).wait_recv()
        part = dot3(inverse, stf[:, lanes(c)])
        rt[:, lanes(c)] = part
        high, low = split(part)
        rcut[:RANK, lanes(c)] = high
        rcut[RANK : 2 * RANK, lanes(c)] = high
        rcut[2 * RANK :, lanes(c)] = low
        for i in range(CHUNKS[c][1] // RANK):
            tile = part[:, i * RANK : (i + 1) * RANK]
            squares += tile * tile
    sq_send[...] = jnp.broadcast_to(jnp.sum(squares.T, axis=0, keepdims=True), sq_send.shape)

    def q_copy(to, slot):
        return pltpu.make_async_remote_copy(
            src_ref=sq_send, dst_ref=sq_in.at[slot], send_sem=q_send.at[to], recv_sem=q_recv.at[slot],
            device_id=(row, to), device_id_type=MESH)

    def q_start(k, _):
        q_copy((col + k) % COL_DEVS, col).start()
        return 0

    lax.fori_loop(1, COL_DEVS, q_start, 0)

    def momentum(i, _):
        rows = pl.ds(pl.multiple_of(i * GROUP, GROUP), GROUP)
        nm[rows, :] = nm[rows, :] - 0.2 * dot(ortho[rows, :].astype(BF16), rcut[:RANK, :])
        return 0

    lax.fori_loop(0, GROUPS, momentum, 0)

    def q_sum(k, acc):
        src = (col + k) % COL_DEVS
        q_copy(src, src).wait_recv()
        return acc + sq_in[src]

    sq[...] = lax.fori_loop(1, COL_DEVS, q_sum, sq_send[...])

    w_copy.wait()

    def sent(k, _):
        to = (col + k) % COL_DEVS
        rs_copy(to, col).wait_send()
        ag_copy(to, col).wait_send()
        q_copy(to, col).wait_send()
        return 0

    lax.fori_loop(1, COL_DEVS, sent, 0)
    for c in range(NCH):
        for cp in (core_copy(c), pair_copy(c)) + first_copies(c) + second_copies(c):
            cp.wait_send()


def final_kernel(nm, wv, ortho, rt, rcut, sq, new_w, new_m, new_r, out, r_out, m_sem, w_sem, r_sem):
    m_copy = pltpu.make_async_copy(nm, new_m, m_sem)
    m_copy.start()
    scale = jnp.sqrt(F32(COLS)) / jnp.sqrt(sq[:1, :] + 1e-06)
    factor = 0.5 * jnp.sqrt(F32(ROWS) / F32(RANK))

    def w_copy(i):
        rows = pl.ds(pl.multiple_of(i * GROUP, GROUP), GROUP)
        return pltpu.make_async_copy(out.at[rows, :], new_w.at[rows, :], w_sem.at[i])

    def weight(i, _):
        rows = pl.ds(pl.multiple_of(i * GROUP, GROUP), GROUP)
        high, low = split(ortho[rows, :] * (scale * factor))
        step = dot(jnp.concatenate([high, low], axis=1), rcut[: 2 * RANK, :]) + dot(high, rcut[2 * RANK :, :])
        out[rows, :] = (wv[rows, :].astype(F32) - step).astype(BF16)
        w_copy(i).start()
        return 0

    lax.fori_loop(0, GROUPS, weight, 0)
    r_out[...] = rt[...].T * scale
    r_copy = pltpu.make_async_copy(r_out, new_r, r_sem)
    r_copy.start()

    def done(i, _):
        w_copy(i).wait()
        return 0

    lax.fori_loop(0, GROUPS, done, 0)
    m_copy.wait()
    r_copy.wait()


def shards(weight, momentum, gradient, right_factor):
    hbm = pl.BlockSpec(memory_space=pltpu.HBM)
    vmem = pl.BlockSpec(memory_space=pltpu.VMEM)
    dma = pltpu.SemaphoreType.DMA
    held = pl.pallas_call(
        main_kernel,
        out_shape=(
            pltpu.VMEM((MY_ROWS, MY_COLS), F32),
            pltpu.VMEM((MY_ROWS, MY_COLS), BF16),
            pltpu.VMEM((MY_ROWS, RANK), F32),
            pltpu.VMEM((RANK, MY_COLS), F32),
            pltpu.VMEM((3 * RANK, MY_COLS), BF16),
            pltpu.VMEM((8, RANK), F32),
        ),
        in_specs=[hbm] * 4,
        out_specs=(vmem,) * 6,
        scratch_shapes=[
            pltpu.VMEM((MY_ROWS, MY_COLS), BF16),
            pltpu.VMEM((MY_ROWS, MY_COLS), BF16),
            pltpu.VMEM((MY_ROWS, MY_COLS), BF16),
            pltpu.VMEM((MY_COLS, RANK), F32),
            pltpu.VMEM((MY_COLS, 2 * RANK), BF16),
            pltpu.VMEM((MY_ROWS, RANK), F32),
            pltpu.VMEM((COL_DEVS, OWN, RANK), F32),
            pltpu.VMEM((MY_ROWS, RANK), F32),
            pltpu.VMEM((2 * RANK, MY_ROWS), BF16),
            pltpu.VMEM((RANK, RANK), F32),
            pltpu.VMEM((ROW_DEVS, GRAM_OWN, RANK), F32),
            pltpu.VMEM((RANK, RANK), F32),
            pltpu.VMEM((RANK, MY_COLS), F32),
            pltpu.VMEM((HALF, MY_COLS), F32),
            pltpu.VMEM((HALF, MY_COLS), F32),
            pltpu.VMEM((HALF, MY_COLS), F32),
            pltpu.VMEM((HALF, MY_COLS), F32),
            pltpu.VMEM((HALF, MY_COLS), F32),
            pltpu.VMEM((RANK, MY_COLS), F32),
            pltpu.VMEM((8, RANK), F32),
            pltpu.VMEM((COL_DEVS, 8, RANK), F32),
            dma((2,)), dma((GROUPS,)), dma((GROUPS,)),
            dma((COL_DEVS,)), dma((COL_DEVS,)), dma((COL_DEVS,)), dma((COL_DEVS,)),
            dma((ROW_DEVS,)), dma((ROW_DEVS,)), dma((ROW_DEVS,)), dma((ROW_DEVS,)),
            dma((NCH, KINDS)), dma((NCH, KINDS)),
            dma((COL_DEVS,)), dma((COL_DEVS,)),
        ],
        compiler_params=pltpu.CompilerParams(collective_id=0, has_side_effects=True, vmem_limit_bytes=50 << 20),
        name="dion_main",
    )(momentum, gradient, right_factor, weight)
    return pl.pallas_call(
        final_kernel,
        out_shape=(
            jax.ShapeDtypeStruct((MY_ROWS, MY_COLS), BF16),
            jax.ShapeDtypeStruct((MY_ROWS, MY_COLS), F32),
            jax.ShapeDtypeStruct((MY_COLS, RANK), F32),
        ),
        in_specs=[vmem] * 6,
        out_specs=(hbm,) * 3,
        scratch_shapes=[
            pltpu.VMEM((MY_ROWS, MY_COLS), BF16),
            pltpu.VMEM((MY_COLS, RANK), F32),
            dma, dma((GROUPS,)), dma,
        ],
        compiler_params=pltpu.CompilerParams(vmem_limit_bytes=24 << 20),
        name="dion_final",
    )(*held)


def solution(mesh):
    placed = (P("row", "col"), P("row", "col"), P("row", "col"), P("col", None))
    return jax.shard_map(
        shards,
        mesh=mesh,
        in_specs=placed,
        out_specs=(P("row", "col"), P("row", "col"), P("col", None)),
        check_vma=False,
    )
```

```python
import jax
import jax.numpy as jnp
from jax import lax
from jax.experimental import pallas as pl
from jax.experimental.pallas import tpu as pltpu
from jax.sharding import PartitionSpec as P

ROWS = 8192
COLS = 26624
RANK = 128
HI = lax.Precision.HIGHEST
MESH = pl.DeviceIdType.MESH
F32 = jnp.float32
BF16 = jnp.bfloat16

ZS, XS, YS, CORES = 4, 4, 4, 2
COL_DEVS = ZS * XS
ROW_DEVS = YS * CORES
MY_ROWS = ROWS // ROW_DEVS
MY_COLS = COLS // COL_DEVS
OWN = MY_ROWS // COL_DEVS
GROUP = OWN * XS
GROUPS = MY_ROWS // GROUP
HALF = RANK // 2
SHARE = HALF // CORES
PART = SHARE // 2
PIECE = OWN // 2
SPAN = GROUP // 2
CHUNKS = ((0, 896), (896, 768))
NCH = len(CHUNKS)
UNITS = tuple((h, c) for h in range(2) for c in range(NCH))
PIVOTS = 16

CORE, FIRST_A, FIRST_B, SECOND_A, SECOND_B, PAIR = range(6)
KINDS = 6

FAR_FIRST = ((2, 2), (2, 1), (2, 3), (1, 2), (3, 2), (1, 1), (3, 3), (1, 3), (3, 1), (2, 0), (0, 2), (1, 0), (3, 0), (0, 1), (0, 3))


def dot(a, b, precision=None):
    return jnp.dot(a, b, precision=precision, preferred_element_type=F32)


def split(a):
    high = a.astype(BF16)
    return high, (a - high.astype(F32)).astype(BF16)


def dot3(a, b):
    ah, al = split(a)
    bh, bl = split(b)
    return dot(ah, bh) + (dot(ah, bl) + dot(al, bh))


def iota(shape, dim):
    return lax.broadcasted_iota(jnp.int32, shape, dim)


def eliminate(rows, first):
    ri, ci = iota(rows.shape, 0), iota(rows.shape, 1)
    cols = [jnp.broadcast_to(rows[:, first + j : first + j + 1], rows.shape) for j in range(PIVOTS)]
    for k in range(PIVOTS):
        scale = lax.rsqrt(cols[k][k : k + 1, :])
        row = jnp.where(ci[:1] == first + k, scale, rows[k : k + 1, :] * scale)
        mult = jnp.where(ri > k, cols[k] * scale, 0.0)
        cleared = jnp.where((ci == first + k) & (ri > k), 0.0, rows)
        rows = jnp.where(ri == k, row, cleared - mult * row)
        for j in range(k + 1, PIVOTS):
            cols[j] = cols[j] - mult * (cols[j][k : k + 1, :] * scale)
    return jnp.where((ci > ri + first) & (ci < first + PIVOTS), 0.0, rows)


def cholesky_block(work, block):
    first = block * PIVOTS
    after = first + PIVOTS
    done = eliminate(work[first:after, :], first)
    work[first:after, :] = done
    if after < RANK:
        ci = iota(done.shape, 1)
        factor = jnp.where(ci >= after, done, 0.0).T
        rest = work[after:, :]
        cj = iota(rest.shape, 1)
        rest = jnp.where((cj >= first) & (cj < after), 0.0, rest)
        work[after:, :] = rest - dot(factor[after:, :], done, HI)


def main_kernel(
    mom, grad, rf, w,
    nm, wv, ortho, rt, rcut, sq,
    hi, lo, gbuf, rbuf, rcat, psend, prs, pan, pan_t, pt, gram_part, gram_pair, gram_in, gram, sloc, cbuf, y1, in1, y2, in2, stf, sq_send, sq_in,
    load_sem, mom_sem, grad_sem,
    rs_send, rs_recv, ag_send, ag_recv, g_send, g_recv, y_send, y_recv, q_send, q_recv,
):
    row = lax.axis_index("row")
    col = lax.axis_index("col")
    y, core = row // CORES, row % CORES
    z, x = col // XS, col % XS
    pair = (y * CORES + 1 - core, col)
    near = ((y + 1 - 2 * (y % 2)) * CORES + core, col)
    far = ((YS - 1 - y) * CORES + core, col)

    barrier = pltpu.get_barrier_semaphore()

    def greet_col(k, _):
        pl.semaphore_signal(barrier, inc=1, device_id=(row, (col + k) % COL_DEVS), device_id_type=MESH)
        return 0

    lax.fori_loop(1, COL_DEVS, greet_col, 0)
    row_peers = [pair] + [(((y + k) % YS) * CORES + core, col) for k in (2, 1, 3)]
    for peer in row_peers:
        pl.semaphore_signal(barrier, inc=1, device_id=peer, device_id_type=MESH)

    rf_copy = pltpu.make_async_copy(rf, rbuf, load_sem.at[0])
    rf_copy.start()
    g0 = (x + z) % GROUPS

    def group_of(j):
        return (g0 + 1 + j) % GROUPS

    def other(step):
        return (z + step[0]) % ZS * XS + (x + step[1]) % XS

    def load(j):
        rows = pl.ds(pl.multiple_of(group_of(j) * GROUP, GROUP), GROUP)
        return (
            pltpu.make_async_copy(mom.at[rows, :], nm.at[rows, :], mom_sem.at[j]),
            pltpu.make_async_copy(grad.at[rows, :], gbuf.at[rows, :], grad_sem.at[j]),
        )

    for j in range(GROUPS):
        for c in load(j):
            c.start()

    rf_copy.wait()
    rh, rl = split(rbuf[...])
    rcat[:, :RANK] = rh
    rcat[:, RANK:] = rl

    def place(c):
        cz, cx = c // XS, c % XS
        return (cx + cz) % GROUPS * XS + cx

    def own_rows(c):
        return pl.ds(pl.multiple_of(place(c) * OWN, OWN), OWN)

    def rs_copy(to, slot):
        return pltpu.make_async_remote_copy(
            src_ref=psend.at[own_rows(to), :], dst_ref=prs.at[slot], send_sem=rs_send.at[to], recv_sem=rs_recv.at[slot],
            device_id=(row, to), device_id_type=MESH)

    def panel_group(j, _):
        for c in load(j):
            c.wait()
        g = group_of(j)
        rows = pl.ds(pl.multiple_of(g * GROUP, GROUP), GROUP)
        a = nm[rows, :] + gbuf[rows, :].astype(F32)
        nm[rows, :] = a
        ah, al = split(a)
        hi[rows, :] = ah
        lo[rows, :] = al
        p = dot(ah, rcat[...])
        p = p[:, :RANK] + p[:, RANK:] + dot(al, rcat[:, :RANK])
        for t in range(XS):
            at = pl.multiple_of(g * GROUP + t * OWN, OWN)
            psend[pl.ds(at, PIECE), :] = p[t * PIECE : (t + 1) * PIECE]
            psend[pl.ds(at + PIECE, PIECE), :] = p[SPAN + t * PIECE : SPAN + (t + 1) * PIECE]

        @pl.when(j == 0)
        def _():
            pl.semaphore_wait(barrier, COL_DEVS - 1 + len(row_peers))

        for t in range(XS):
            to = ((g + GROUPS - t) % GROUPS) * XS + t

            @pl.when(to != col)
            def _():
                rs_copy(to, col).start()

        return 0

    lax.fori_loop(0, GROUPS, panel_group, 0)
    w_copy = pltpu.make_async_copy(w, wv, load_sem.at[1])
    w_copy.start()

    mine = own_rows(col)

    total = psend[mine, :]
    for step in reversed(FAR_FIRST):
        src = other(step)
        rs_copy(src, src).wait_recv()
        total = total + prs[src]

    def own_block(c):
        return pl.ds(pl.multiple_of(place(c) * PIECE, PIECE), PIECE)

    for h in range(2):
        half = total[:, h * HALF : (h + 1) * HALF]
        pan[h, own_block(col), :] = jnp.concatenate([half[:PIECE], half[PIECE:]], axis=1)

    def ag_copy(h, to, owner):
        block = pan.at[h, own_block(owner), :]
        return pltpu.make_async_remote_copy(
            src_ref=block, dst_ref=block, send_sem=ag_send.at[h, to], recv_sem=ag_recv.at[h, owner],
            device_id=(row, to), device_id_type=MESH)

    for h in range(2):
        for step in FAR_FIRST:
            ag_copy(h, other(step), col).start()

    def arrive(h):
        def group(j, _):
            g = group_of(j)
            for t in range(XS):
                src = (g + GROUPS - t) % GROUPS * XS + t

                @pl.when(src != col)
                def _():
                    ag_copy(h, src, src).wait_recv()

            block = pan[h, pl.ds(pl.multiple_of(g * SPAN, SPAN), SPAN), :].T
            ranks = pl.ds(h * HALF, HALF)
            for i in range(2):
                at = pl.ds(pl.multiple_of(g * GROUP + i * SPAN, SPAN), SPAN)
                piece = block[i * HALF : (i + 1) * HALF]
                high, low = split(piece)
                pan_t[ranks, at] = piece
                pt[h, :HALF, at] = high
                pt[h, HALF:, at] = low
            if h == 1:
                both = pan_t[:, pl.ds(pl.multiple_of(g * GROUP, GROUP), GROUP)]
                gram_part[...] += lax.dot_general(both, both, (((1,), (1,)), ((), ())), precision=HI, preferred_element_type=F32)
            return 0

        lax.fori_loop(0, GROUPS, group, 0)

    gram_part[...] = jnp.zeros_like(gram_part)
    arrive(0)

    ours = pl.ds(pl.multiple_of(core * HALF, HALF), HALF)
    theirs = pl.ds(pl.multiple_of((1 - core) * HALF, HALF), HALF)

    def gram_copy(kind, src, dst, to):
        return pltpu.make_async_remote_copy(
            src_ref=src, dst_ref=dst, send_sem=g_send.at[kind], recv_sem=g_recv.at[kind], device_id=to, device_id_type=MESH)

    gram_scatter = gram_copy(0, gram_part.at[theirs, :], gram_pair, pair)
    gram_gather = gram_copy(1, gram.at[ours, :], gram.at[ours, :], pair)

    def gram_y(to, slot):
        return pltpu.make_async_remote_copy(
            src_ref=gram_in.at[slot], dst_ref=gram_in.at[slot], send_sem=g_send.at[2 + to], recv_sem=g_recv.at[2 + slot],
            device_id=(to * CORES + core, col), device_id_type=MESH)

    def gram_1():
        gram_scatter.wait_recv()
        gram_in[y] = gram_part[ours, :] + gram_pair[...]
        for k in (2, 1, 3):
            gram_y((y + k) % YS, y).start()

    def gram_2():
        for k in (1, 3, 2):
            src = (y + k) % YS
            gram_y(src, src).wait_recv()
        gram[ours, :] = (gram_in[0] + gram_in[1]) + (gram_in[2] + gram_in[3])
        gram_gather.start()

    def ycopy(kind, c, src, dst, to):
        return pltpu.make_async_remote_copy(
            src_ref=src, dst_ref=dst, send_sem=y_send.at[c, kind], recv_sem=y_recv.at[c, kind], device_id=to, device_id_type=MESH)

    def lanes(u):
        return pl.ds(*CHUNKS[UNITS[u][1]])

    def core_copy(u):
        return ycopy(CORE, u, sloc.at[ranks_of(u, 1 - core), lanes(u)], cbuf.at[share(u), lanes(u)], pair)

    def ranks_of(u, c):
        return pl.ds(pl.multiple_of(UNITS[u][0] * HALF + c * SHARE, SHARE), SHARE)

    def share(u):
        return pl.ds(UNITS[u][0] * SHARE, SHARE)

    def part_rows(u, part):
        return pl.ds(UNITS[u][0] * SHARE + part * PART, PART)

    def first_copies(u):
        return (
            ycopy(FIRST_A, u, y1.at[part_rows(u, 0), lanes(u)], in1.at[part_rows(u, 0), lanes(u)], near),
            ycopy(FIRST_B, u, y1.at[part_rows(u, 1), lanes(u)], in1.at[part_rows(u, 1), lanes(u)], far),
        )

    def second_copies(u):
        return (
            ycopy(SECOND_A, u, y2.at[part_rows(u, 0), lanes(u)], in2.at[part_rows(u, 0), lanes(u)], far),
            ycopy(SECOND_B, u, y2.at[part_rows(u, 1), lanes(u)], in2.at[part_rows(u, 1), lanes(u)], near),
        )

    def pair_copy(u):
        block = stf.at[ranks_of(u, core), lanes(u)]
        return ycopy(PAIR, u, block, block, pair)

    def product(u):
        h = UNITS[u][0]
        t = dot(pt[h], hi[:, lanes(u)])
        sloc[pl.ds(h * HALF, HALF), lanes(u)] = t[:HALF] + t[HALF:] + dot(pt[h, :HALF, :], lo[:, lanes(u)])
        core_copy(u).start()

    def first(u):
        core_copy(u).wait_recv()
        y1[share(u), lanes(u)] = sloc[ranks_of(u, core), lanes(u)] + cbuf[share(u), lanes(u)]
        for cp in first_copies(u):
            cp.start()

    def second(u):
        for part, cp in enumerate(first_copies(u)):
            cp.wait_recv()
            at = part_rows(u, part)
            y2[at, lanes(u)] = y1[at, lanes(u)] + in1[at, lanes(u)]
            second_copies(u)[part].start()

    def third(u):
        for cp in second_copies(u):
            cp.wait_recv()
        stf[ranks_of(u, core), lanes(u)] = y2[share(u), lanes(u)] + in2[share(u), lanes(u)]
        pair_copy(u).start()

    product(0)
    product(1)
    first(0)
    first(1)
    arrive(1)
    gram_scatter.start()
    product(2)
    product(3)
    gram_1()
    first(2)
    first(3)
    second(0)
    second(1)

    gram_2()
    second(2)
    gram_scatter.wait_send()
    gram_gather.wait()
    steps = {0: (second, 3), 2: (third, 0), 3: (third, 1), 5: (third, 2), 6: (third, 3)}
    for b in range(RANK // PIVOTS):
        cholesky_block(gram, b)
        if b in steps:
            move, u = steps[b]
            move(u)
    inverse = jnp.where(iota((RANK, RANK), 0) >= iota((RANK, RANK), 1), gram[...], 0.0)

    squares = jnp.zeros((RANK, RANK), F32)
    for c in range(NCH):
        pair_copy(c).wait_recv()
        pair_copy(NCH + c).wait_recv()
        part = dot3(inverse, stf[:, lanes(c)])
        rt[:, lanes(c)] = part
        for i in range(CHUNKS[c][1] // RANK):
            tile = part[:, i * RANK : (i + 1) * RANK]
            squares += tile * tile
    sq_send[...] = jnp.broadcast_to(jnp.sum(squares.T, axis=0, keepdims=True), sq_send.shape)

    def q_copy(to, slot):
        return pltpu.make_async_remote_copy(
            src_ref=sq_send, dst_ref=sq_in.at[slot], send_sem=q_send.at[to], recv_sem=q_recv.at[slot],
            device_id=(row, to), device_id_type=MESH)

    for step in FAR_FIRST:
        q_copy(other(step), col).start()

    ortho[...] = dot3(inverse, pan_t[...]).T
    high, low = split(rt[...])
    rcut[:RANK, :] = high
    rcut[RANK : 2 * RANK, :] = high
    rcut[2 * RANK :, :] = low

    def momentum(i, _):
        rows = pl.ds(pl.multiple_of(i * GROUP, GROUP), GROUP)
        nm[rows, :] = nm[rows, :] - 0.2 * dot(ortho[rows, :].astype(BF16), rcut[:RANK, :])
        return 0

    lax.fori_loop(0, GROUPS, momentum, 0)

    w_copy.wait()

    def sent(k, _):
        to = (col + k) % COL_DEVS
        rs_copy(to, col).wait_send()
        ag_copy(0, to, col).wait_send()
        ag_copy(1, to, col).wait_send()
        return 0

    lax.fori_loop(1, COL_DEVS, sent, 0)
    for k in (1, 2, 3):
        gram_y((y + k) % YS, y).wait_send()
    for u in range(len(UNITS)):
        for cp in (core_copy(u), pair_copy(u)) + first_copies(u) + second_copies(u):
            cp.wait_send()

    total = sq_send[...]
    for step in reversed(FAR_FIRST):
        src = other(step)
        q_copy(src, src).wait_recv()
        total = total + sq_in[src]
    sq[...] = total

    def q_sent(k, _):
        q_copy((col + k) % COL_DEVS, col).wait_send()
        return 0

    lax.fori_loop(1, COL_DEVS, q_sent, 0)


def final_kernel(nm, wv, ortho, rt, rcut, sq, new_w, new_m, new_r, out, r_out, m_sem, w_sem, r_sem):
    m_copy = pltpu.make_async_copy(nm, new_m, m_sem)
    m_copy.start()
    scale = jnp.sqrt(F32(COLS)) / jnp.sqrt(sq[:1, :] + 1e-06)
    factor = 0.5 * jnp.sqrt(F32(ROWS) / F32(RANK))

    def w_copy(i):
        rows = pl.ds(pl.multiple_of(i * GROUP, GROUP), GROUP)
        return pltpu.make_async_copy(out.at[rows, :], new_w.at[rows, :], w_sem.at[i])

    def weight(i, _):
        rows = pl.ds(pl.multiple_of(i * GROUP, GROUP), GROUP)
        high, low = split(ortho[rows, :] * (scale * factor))
        step = dot(jnp.concatenate([high, low], axis=1), rcut[: 2 * RANK, :]) + dot(high, rcut[2 * RANK :, :])
        out[rows, :] = (wv[rows, :].astype(F32) - step).astype(BF16)
        w_copy(i).start()
        return 0

    lax.fori_loop(0, GROUPS, weight, 0)
    r_out[...] = rt[...].T * scale
    r_copy = pltpu.make_async_copy(r_out, new_r, r_sem)
    r_copy.start()

    def done(i, _):
        w_copy(i).wait()
        return 0

    lax.fori_loop(0, GROUPS, done, 0)
    m_copy.wait()
    r_copy.wait()


def shards(weight, momentum, gradient, right_factor):
    hbm = pl.BlockSpec(memory_space=pltpu.HBM)
    vmem = pl.BlockSpec(memory_space=pltpu.VMEM)
    dma = pltpu.SemaphoreType.DMA
    held = pl.pallas_call(
        main_kernel,
        out_shape=(
            pltpu.VMEM((MY_ROWS, MY_COLS), F32),
            pltpu.VMEM((MY_ROWS, MY_COLS), BF16),
            pltpu.VMEM((MY_ROWS, RANK), F32),
            pltpu.VMEM((RANK, MY_COLS), F32),
            pltpu.VMEM((3 * RANK, MY_COLS), BF16),
            pltpu.VMEM((8, RANK), F32),
        ),
        in_specs=[hbm] * 4,
        out_specs=(vmem,) * 6,
        scratch_shapes=[
            pltpu.VMEM((MY_ROWS, MY_COLS), BF16),
            pltpu.VMEM((MY_ROWS, MY_COLS), BF16),
            pltpu.VMEM((MY_ROWS, MY_COLS), BF16),
            pltpu.VMEM((MY_COLS, RANK), F32),
            pltpu.VMEM((MY_COLS, 2 * RANK), BF16),
            pltpu.VMEM((MY_ROWS, RANK), F32),
            pltpu.VMEM((COL_DEVS, OWN, RANK), F32),
            pltpu.VMEM((2, MY_ROWS // 2, RANK), F32),
            pltpu.VMEM((RANK, MY_ROWS), F32),
            pltpu.VMEM((2, RANK, MY_ROWS), BF16),
            pltpu.VMEM((RANK, RANK), F32),
            pltpu.VMEM((HALF, RANK), F32),
            pltpu.VMEM((YS, HALF, RANK), F32),
            pltpu.VMEM((RANK, RANK), F32),
            pltpu.VMEM((RANK, MY_COLS), F32),
            pltpu.VMEM((HALF, MY_COLS), F32),
            pltpu.VMEM((HALF, MY_COLS), F32),
            pltpu.VMEM((HALF, MY_COLS), F32),
            pltpu.VMEM((HALF, MY_COLS), F32),
            pltpu.VMEM((HALF, MY_COLS), F32),
            pltpu.VMEM((RANK, MY_COLS), F32),
            pltpu.VMEM((8, RANK), F32),
            pltpu.VMEM((COL_DEVS, 8, RANK), F32),
            dma((2,)), dma((GROUPS,)), dma((GROUPS,)),
            dma((COL_DEVS,)), dma((COL_DEVS,)), dma((2, COL_DEVS)), dma((2, COL_DEVS)),
            dma((2 + YS,)), dma((2 + YS,)),
            dma((len(UNITS), KINDS)), dma((len(UNITS), KINDS)),
            dma((COL_DEVS,)), dma((COL_DEVS,)),
        ],
        compiler_params=pltpu.CompilerParams(collective_id=0, has_side_effects=True, vmem_limit_bytes=50 << 20),
        name="dion_main",
    )(momentum, gradient, right_factor, weight)
    return pl.pallas_call(
        final_kernel,
        out_shape=(
            jax.ShapeDtypeStruct((MY_ROWS, MY_COLS), BF16),
            jax.ShapeDtypeStruct((MY_ROWS, MY_COLS), F32),
            jax.ShapeDtypeStruct((MY_COLS, RANK), F32),
        ),
        in_specs=[vmem] * 6,
        out_specs=(hbm,) * 3,
        scratch_shapes=[
            pltpu.VMEM((MY_ROWS, MY_COLS), BF16),
            pltpu.VMEM((MY_COLS, RANK), F32),
            dma, dma((GROUPS,)), dma,
        ],
        compiler_params=pltpu.CompilerParams(vmem_limit_bytes=24 << 20),
        name="dion_final",
    )(*held)


def solution(mesh):
    placed = (P("row", "col"), P("row", "col"), P("row", "col"), P("col", None))
    return jax.shard_map(
        shards,
        mesh=mesh,
        in_specs=placed,
        out_specs=(P("row", "col"), P("row", "col"), P("col", None)),
        check_vma=False,
    )
```

```python
import jax
import jax.numpy as jnp
from jax import lax
from jax.experimental import pallas as pl
from jax.experimental.pallas import tpu as pltpu
from jax.sharding import PartitionSpec as P

ROWS = 8192
COLS = 26624
RANK = 128
HI = lax.Precision.HIGHEST
MESH = pl.DeviceIdType.MESH
F32 = jnp.float32
BF16 = jnp.bfloat16

ZS, XS, YS, CORES = 4, 4, 4, 2
COL_DEVS = ZS * XS
ROW_DEVS = YS * CORES
MY_ROWS = ROWS // ROW_DEVS
MY_COLS = COLS // COL_DEVS
OWN = MY_ROWS // COL_DEVS
GROUP = OWN * XS
GROUPS = MY_ROWS // GROUP
HALF = RANK // 2
SHARE = HALF // CORES
PART = SHARE // 2
PIECE = OWN // 2
SPAN = GROUP // 2
UNITS = ((0, 0, 896), (0, 896, 768), (1, 0, 512), (1, 512, 512), (1, 1024, 640))
LATE = (2, 3, 4)
PIVOTS = 16

CORE, FIRST_A, FIRST_B, SECOND_A, SECOND_B, PAIR = range(6)
KINDS = 6

FAR_FIRST = ((2, 2), (2, 1), (2, 3), (1, 2), (3, 2), (1, 1), (3, 3), (1, 3), (3, 1), (2, 0), (0, 2), (1, 0), (3, 0), (0, 1), (0, 3))


def dot(a, b, precision=None):
    return jnp.dot(a, b, precision=precision, preferred_element_type=F32)


def split(a):
    high = a.astype(BF16)
    return high, (a - high.astype(F32)).astype(BF16)


def dot3(a, b):
    ah, al = split(a)
    bh, bl = split(b)
    return dot(ah, bh) + (dot(ah, bl) + dot(al, bh))


def iota(shape, dim):
    return lax.broadcasted_iota(jnp.int32, shape, dim)


def eliminate(rows, first):
    ri, ci = iota(rows.shape, 0), iota(rows.shape, 1)
    cols = [jnp.broadcast_to(rows[:, first + j : first + j + 1], rows.shape) for j in range(PIVOTS)]
    for k in range(PIVOTS):
        scale = lax.rsqrt(cols[k][k : k + 1, :])
        row = jnp.where(ci[:1] == first + k, scale, rows[k : k + 1, :] * scale)
        mult = jnp.where(ri > k, cols[k] * scale, 0.0)
        cleared = jnp.where((ci == first + k) & (ri > k), 0.0, rows)
        rows = jnp.where(ri == k, row, cleared - mult * row)
        for j in range(k + 1, PIVOTS):
            cols[j] = cols[j] - mult * (cols[j][k : k + 1, :] * scale)
    return jnp.where((ci > ri + first) & (ci < first + PIVOTS), 0.0, rows)


def cholesky_block(work, block):
    first = block * PIVOTS
    after = first + PIVOTS
    done = eliminate(work[first:after, :], first)
    work[first:after, :] = done
    if after < RANK:
        ci = iota(done.shape, 1)
        factor = jnp.where(ci >= after, done, 0.0).T
        rest = work[after:, :]
        cj = iota(rest.shape, 1)
        rest = jnp.where((cj >= first) & (cj < after), 0.0, rest)
        work[after:, :] = rest - dot(factor[after:, :], done, HI)


def main_kernel(
    mom, grad, rf, w,
    nm, wv, ortho, rt, rcut, sq,
    hi, lo, gbuf, rbuf, rcat, psend, prs, pan, pan_t, pt, gram_part, gram_pair, gram_in, gram, sloc, cbuf, y1, in1, y2, in2, stf, sq_send, sq_in,
    load_sem, mom_sem, grad_sem,
    rs_send, rs_recv, ag_send, ag_recv, g_send, g_recv, y_send, y_recv, q_send, q_recv,
):
    row = lax.axis_index("row")
    col = lax.axis_index("col")
    y, core = row // CORES, row % CORES
    z, x = col // XS, col % XS
    pair = (y * CORES + 1 - core, col)
    near = ((y + 1 - 2 * (y % 2)) * CORES + core, col)
    far = ((YS - 1 - y) * CORES + core, col)

    rf_copy = pltpu.make_async_copy(rf, rbuf, load_sem.at[0])
    rf_copy.start()
    g0 = (x + z) % GROUPS

    def group_of(j):
        return (g0 + 1 + j) % GROUPS

    def other(step):
        return (z + step[0]) % ZS * XS + (x + step[1]) % XS

    def load(j):
        rows = pl.ds(pl.multiple_of(group_of(j) * GROUP, GROUP), GROUP)
        return (
            pltpu.make_async_copy(mom.at[rows, :], nm.at[rows, :], mom_sem.at[j]),
            pltpu.make_async_copy(grad.at[rows, :], gbuf.at[rows, :], grad_sem.at[j]),
        )

    for c in load(0):
        c.start()

    barrier = pltpu.get_barrier_semaphore()

    def greet_col(k, _):
        pl.semaphore_signal(barrier, inc=1, device_id=(row, (col + k) % COL_DEVS), device_id_type=MESH)
        return 0

    lax.fori_loop(1, COL_DEVS, greet_col, 0)
    row_peers = [pair] + [(((y + k) % YS) * CORES + core, col) for k in (2, 1, 3)]
    for peer in row_peers:
        pl.semaphore_signal(barrier, inc=1, device_id=peer, device_id_type=MESH)

    for j in range(1, GROUPS):
        for c in load(j):
            c.start()

    rf_copy.wait()
    rh, rl = split(rbuf[...])
    rcat[:, :RANK] = rh
    rcat[:, RANK:] = rl

    def place(c):
        cz, cx = c // XS, c % XS
        return (cx + cz) % GROUPS * XS + cx

    def own_rows(c):
        return pl.ds(pl.multiple_of(place(c) * OWN, OWN), OWN)

    def rs_copy(to, slot):
        return pltpu.make_async_remote_copy(
            src_ref=psend.at[own_rows(to), :], dst_ref=prs.at[slot], send_sem=rs_send.at[to], recv_sem=rs_recv.at[slot],
            device_id=(row, to), device_id_type=MESH)

    def panel_group(j, _):
        for c in load(j):
            c.wait()
        g = group_of(j)
        rows = pl.ds(pl.multiple_of(g * GROUP, GROUP), GROUP)
        a = nm[rows, :] + gbuf[rows, :].astype(F32)
        nm[rows, :] = a
        ah, al = split(a)
        hi[rows, :] = ah
        lo[rows, :] = al
        p = dot(ah, rcat[...])
        p = p[:, :RANK] + p[:, RANK:] + dot(al, rcat[:, :RANK])
        for t in range(XS):
            at = pl.multiple_of(g * GROUP + t * OWN, OWN)
            psend[pl.ds(at, PIECE), :] = p[t * PIECE : (t + 1) * PIECE]
            psend[pl.ds(at + PIECE, PIECE), :] = p[SPAN + t * PIECE : SPAN + (t + 1) * PIECE]

        @pl.when(j == 0)
        def _():
            pl.semaphore_wait(barrier, COL_DEVS - 1 + len(row_peers))

        for t in range(XS):
            to = ((g + GROUPS - t) % GROUPS) * XS + t

            @pl.when(to != col)
            def _():
                rs_copy(to, col).start()

        return 0

    lax.fori_loop(0, GROUPS, panel_group, 0)
    w_copy = pltpu.make_async_copy(w, wv, load_sem.at[1])
    w_copy.start()

    mine = own_rows(col)

    total = psend[mine, :]
    for step in reversed(FAR_FIRST):
        src = other(step)
        rs_copy(src, src).wait_recv()
        total = total + prs[src]

    def own_block(c):
        return pl.ds(pl.multiple_of(place(c) * PIECE, PIECE), PIECE)

    for h in range(2):
        half = total[:, h * HALF : (h + 1) * HALF]
        pan[h, own_block(col), :] = jnp.concatenate([half[:PIECE], half[PIECE:]], axis=1)

    def ag_copy(h, to, owner):
        block = pan.at[h, own_block(owner), :]
        return pltpu.make_async_remote_copy(
            src_ref=block, dst_ref=block, send_sem=ag_send.at[h, to], recv_sem=ag_recv.at[h, owner],
            device_id=(row, to), device_id_type=MESH)

    for h in range(2):
        for step in FAR_FIRST:
            ag_copy(h, other(step), col).start()

    def arrive(h):
        for step in reversed(FAR_FIRST):
            src = other(step)
            ag_copy(h, src, src).wait_recv()
        block = pan[h].T
        for g in range(GROUPS):
            for i in range(2):
                at = pl.ds(g * GROUP + i * SPAN, SPAN)
                piece = block[i * HALF : (i + 1) * HALF, g * SPAN : (g + 1) * SPAN]
                high, low = split(piece)
                pan_t[h * HALF : (h + 1) * HALF, at] = piece
                pt[h, :HALF, at] = high
                pt[h, HALF:, at] = low

    arrive(0)

    ours = pl.ds(pl.multiple_of(core * HALF, HALF), HALF)
    theirs = pl.ds(pl.multiple_of((1 - core) * HALF, HALF), HALF)

    def gram_copy(kind, src, dst, to):
        return pltpu.make_async_remote_copy(
            src_ref=src, dst_ref=dst, send_sem=g_send.at[kind], recv_sem=g_recv.at[kind], device_id=to, device_id_type=MESH)

    gram_scatter = gram_copy(0, gram_part.at[theirs, :], gram_pair, pair)
    gram_gather = gram_copy(1, gram.at[ours, :], gram.at[ours, :], pair)

    def gram_y(to, slot):
        return pltpu.make_async_remote_copy(
            src_ref=gram_in.at[slot], dst_ref=gram_in.at[slot], send_sem=g_send.at[2 + to], recv_sem=g_recv.at[2 + slot],
            device_id=(to * CORES + core, col), device_id_type=MESH)

    def gram_1():
        gram_scatter.wait_recv()
        gram_in[y] = gram_part[ours, :] + gram_pair[...]
        for k in (2, 1, 3):
            gram_y((y + k) % YS, y).start()

    def gram_2():
        for k in (1, 3, 2):
            src = (y + k) % YS
            gram_y(src, src).wait_recv()
        gram[ours, :] = (gram_in[0] + gram_in[1]) + (gram_in[2] + gram_in[3])
        gram_gather.start()

    def ycopy(kind, c, src, dst, to):
        return pltpu.make_async_remote_copy(
            src_ref=src, dst_ref=dst, send_sem=y_send.at[c, kind], recv_sem=y_recv.at[c, kind], device_id=to, device_id_type=MESH)

    def lanes(u):
        return pl.ds(*UNITS[u][1:])

    def core_copy(u):
        return ycopy(CORE, u, sloc.at[ranks_of(u, 1 - core), lanes(u)], cbuf.at[share(u), lanes(u)], pair)

    def ranks_of(u, c):
        return pl.ds(pl.multiple_of(UNITS[u][0] * HALF + c * SHARE, SHARE), SHARE)

    def share(u):
        return pl.ds(UNITS[u][0] * SHARE, SHARE)

    def part_rows(u, part):
        return pl.ds(UNITS[u][0] * SHARE + part * PART, PART)

    def first_copies(u):
        return (
            ycopy(FIRST_A, u, y1.at[part_rows(u, 0), lanes(u)], in1.at[part_rows(u, 0), lanes(u)], near),
            ycopy(FIRST_B, u, y1.at[part_rows(u, 1), lanes(u)], in1.at[part_rows(u, 1), lanes(u)], far),
        )

    def second_copies(u):
        return (
            ycopy(SECOND_A, u, y2.at[part_rows(u, 0), lanes(u)], in2.at[part_rows(u, 0), lanes(u)], far),
            ycopy(SECOND_B, u, y2.at[part_rows(u, 1), lanes(u)], in2.at[part_rows(u, 1), lanes(u)], near),
        )

    def pair_copy(u):
        block = stf.at[ranks_of(u, core), lanes(u)]
        return ycopy(PAIR, u, block, block, pair)

    def product(u):
        h = UNITS[u][0]
        t = dot(pt[h], hi[:, lanes(u)])
        sloc[pl.ds(h * HALF, HALF), lanes(u)] = t[:HALF] + t[HALF:] + dot(pt[h, :HALF, :], lo[:, lanes(u)])
        core_copy(u).start()

    def first(u):
        core_copy(u).wait_recv()
        y1[share(u), lanes(u)] = sloc[ranks_of(u, core), lanes(u)] + cbuf[share(u), lanes(u)]
        for cp in first_copies(u):
            cp.start()

    def second(u):
        for part, cp in enumerate(first_copies(u)):
            cp.wait_recv()
            at = part_rows(u, part)
            y2[at, lanes(u)] = y1[at, lanes(u)] + in1[at, lanes(u)]
            second_copies(u)[part].start()

    def third(u):
        for cp in second_copies(u):
            cp.wait_recv()
        stf[ranks_of(u, core), lanes(u)] = y2[share(u), lanes(u)] + in2[share(u), lanes(u)]
        pair_copy(u).start()

    product(0)
    product(1)
    first(0)
    first(1)
    arrive(1)
    gram_part[...] = lax.dot_general(pan_t[...], pan_t[...], (((1,), (1,)), ((), ())), precision=HI, preferred_element_type=F32)
    gram_scatter.start()
    product(2)
    product(3)
    product(4)
    gram_1()
    first(2)
    first(3)
    first(4)
    second(0)
    second(1)
    second(2)

    gram_2()
    second(3)
    second(4)
    gram_scatter.wait_send()
    gram_gather.wait()
    steps = {2: (third, 0), 3: (third, 1), 4: (third, 2), 5: (third, 3), 6: (third, 4)}
    for b in range(RANK // PIVOTS):
        cholesky_block(gram, b)
        if b in steps:
            move, u = steps[b]
            move(u)
    inverse = jnp.where(iota((RANK, RANK), 0) >= iota((RANK, RANK), 1), gram[...], 0.0)

    squares = jnp.zeros((RANK, RANK), F32)
    for u in range(LATE[0]):
        pair_copy(u).wait_recv()
    for u in LATE:
        pair_copy(u).wait_recv()
        part = dot3(inverse, stf[:, lanes(u)])
        rt[:, lanes(u)] = part
        for i in range(UNITS[u][2] // RANK):
            tile = part[:, i * RANK : (i + 1) * RANK]
            squares += tile * tile
    sq_send[...] = jnp.broadcast_to(jnp.sum(squares.T, axis=0, keepdims=True), sq_send.shape)

    def q_copy(to, slot):
        return pltpu.make_async_remote_copy(
            src_ref=sq_send, dst_ref=sq_in.at[slot], send_sem=q_send.at[to], recv_sem=q_recv.at[slot],
            device_id=(row, to), device_id_type=MESH)

    for step in FAR_FIRST:
        q_copy(other(step), col).start()

    ortho[...] = dot3(inverse, pan_t[...]).T
    high, low = split(rt[...])
    rcut[:RANK, :] = high
    rcut[RANK : 2 * RANK, :] = high
    rcut[2 * RANK :, :] = low

    def momentum(i, _):
        rows = pl.ds(pl.multiple_of(i * GROUP, GROUP), GROUP)
        nm[rows, :] = nm[rows, :] - 0.2 * dot(ortho[rows, :].astype(BF16), rcut[:RANK, :])
        return 0

    lax.fori_loop(0, GROUPS, momentum, 0)

    w_copy.wait()

    def sent(k, _):
        to = (col + k) % COL_DEVS
        rs_copy(to, col).wait_send()
        ag_copy(0, to, col).wait_send()
        ag_copy(1, to, col).wait_send()
        return 0

    lax.fori_loop(1, COL_DEVS, sent, 0)
    for k in (1, 2, 3):
        gram_y((y + k) % YS, y).wait_send()
    for u in range(len(UNITS)):
        for cp in (core_copy(u), pair_copy(u)) + first_copies(u) + second_copies(u):
            cp.wait_send()

    total = sq_send[...]
    for step in reversed(FAR_FIRST):
        src = other(step)
        q_copy(src, src).wait_recv()
        total = total + sq_in[src]
    sq[...] = total

    def q_sent(k, _):
        q_copy((col + k) % COL_DEVS, col).wait_send()
        return 0

    lax.fori_loop(1, COL_DEVS, q_sent, 0)


def final_kernel(nm, wv, ortho, rt, rcut, sq, new_w, new_m, new_r, out, r_out, m_sem, w_sem, r_sem):
    m_copy = pltpu.make_async_copy(nm, new_m, m_sem)
    m_copy.start()
    scale = jnp.sqrt(F32(COLS)) / jnp.sqrt(sq[:1, :] + 1e-06)
    factor = 0.5 * jnp.sqrt(F32(ROWS) / F32(RANK))

    def w_copy(i):
        rows = pl.ds(pl.multiple_of(i * GROUP, GROUP), GROUP)
        return pltpu.make_async_copy(out.at[rows, :], new_w.at[rows, :], w_sem.at[i])

    def weight(i, _):
        rows = pl.ds(pl.multiple_of(i * GROUP, GROUP), GROUP)
        high, low = split(ortho[rows, :] * (scale * factor))
        step = dot(jnp.concatenate([high, low], axis=1), rcut[: 2 * RANK, :]) + dot(high, rcut[2 * RANK :, :])
        out[rows, :] = (wv[rows, :].astype(F32) - step).astype(BF16)
        w_copy(i).start()
        return 0

    lax.fori_loop(0, GROUPS, weight, 0)
    r_out[...] = rt[...].T * scale
    r_copy = pltpu.make_async_copy(r_out, new_r, r_sem)
    r_copy.start()

    def done(i, _):
        w_copy(i).wait()
        return 0

    lax.fori_loop(0, GROUPS, done, 0)
    m_copy.wait()
    r_copy.wait()


def shards(weight, momentum, gradient, right_factor):
    hbm = pl.BlockSpec(memory_space=pltpu.HBM)
    vmem = pl.BlockSpec(memory_space=pltpu.VMEM)
    dma = pltpu.SemaphoreType.DMA
    held = pl.pallas_call(
        main_kernel,
        out_shape=(
            pltpu.VMEM((MY_ROWS, MY_COLS), F32),
            pltpu.VMEM((MY_ROWS, MY_COLS), BF16),
            pltpu.VMEM((MY_ROWS, RANK), F32),
            pltpu.VMEM((RANK, MY_COLS), F32),
            pltpu.VMEM((3 * RANK, MY_COLS), BF16),
            pltpu.VMEM((8, RANK), F32),
        ),
        in_specs=[hbm] * 4,
        out_specs=(vmem,) * 6,
        scratch_shapes=[
            pltpu.VMEM((MY_ROWS, MY_COLS), BF16),
            pltpu.VMEM((MY_ROWS, MY_COLS), BF16),
            pltpu.VMEM((MY_ROWS, MY_COLS), BF16),
            pltpu.VMEM((MY_COLS, RANK), F32),
            pltpu.VMEM((MY_COLS, 2 * RANK), BF16),
            pltpu.VMEM((MY_ROWS, RANK), F32),
            pltpu.VMEM((COL_DEVS, OWN, RANK), F32),
            pltpu.VMEM((2, MY_ROWS // 2, RANK), F32),
            pltpu.VMEM((RANK, MY_ROWS), F32),
            pltpu.VMEM((2, RANK, MY_ROWS), BF16),
            pltpu.VMEM((RANK, RANK), F32),
            pltpu.VMEM((HALF, RANK), F32),
            pltpu.VMEM((YS, HALF, RANK), F32),
            pltpu.VMEM((RANK, RANK), F32),
            pltpu.VMEM((RANK, MY_COLS), F32),
            pltpu.VMEM((HALF, MY_COLS), F32),
            pltpu.VMEM((HALF, MY_COLS), F32),
            pltpu.VMEM((HALF, MY_COLS), F32),
            pltpu.VMEM((HALF, MY_COLS), F32),
            pltpu.VMEM((HALF, MY_COLS), F32),
            pltpu.VMEM((RANK, MY_COLS), F32),
            pltpu.VMEM((8, RANK), F32),
            pltpu.VMEM((COL_DEVS, 8, RANK), F32),
            dma((2,)), dma((GROUPS,)), dma((GROUPS,)),
            dma((COL_DEVS,)), dma((COL_DEVS,)), dma((2, COL_DEVS)), dma((2, COL_DEVS)),
            dma((2 + YS,)), dma((2 + YS,)),
            dma((len(UNITS), KINDS)), dma((len(UNITS), KINDS)),
            dma((COL_DEVS,)), dma((COL_DEVS,)),
        ],
        compiler_params=pltpu.CompilerParams(collective_id=0, has_side_effects=True, vmem_limit_bytes=50 << 20),
        name="dion_main",
    )(momentum, gradient, right_factor, weight)
    return pl.pallas_call(
        final_kernel,
        out_shape=(
            jax.ShapeDtypeStruct((MY_ROWS, MY_COLS), BF16),
            jax.ShapeDtypeStruct((MY_ROWS, MY_COLS), F32),
            jax.ShapeDtypeStruct((MY_COLS, RANK), F32),
        ),
        in_specs=[vmem] * 6,
        out_specs=(hbm,) * 3,
        scratch_shapes=[
            pltpu.VMEM((MY_ROWS, MY_COLS), BF16),
            pltpu.VMEM((MY_COLS, RANK), F32),
            dma, dma((GROUPS,)), dma,
        ],
        compiler_params=pltpu.CompilerParams(vmem_limit_bytes=24 << 20),
        name="dion_final",
    )(*held)


def solution(mesh):
    placed = (P("row", "col"), P("row", "col"), P("row", "col"), P("col", None))
    return jax.shard_map(
        shards,
        mesh=mesh,
        in_specs=placed,
        out_specs=(P("row", "col"), P("row", "col"), P("col", None)),
        check_vma=False,
    )
```

```python
import jax
import jax.numpy as jnp
from jax import lax
from jax.experimental import pallas as pl
from jax.experimental.pallas import tpu as pltpu
from jax.sharding import PartitionSpec as P

ROWS = 8192
COLS = 26624
RANK = 128
HI = lax.Precision.HIGHEST
MESH = pl.DeviceIdType.MESH
F32 = jnp.float32
BF16 = jnp.bfloat16

ZS, XS, YS, CORES = 4, 4, 4, 2
COL_DEVS = ZS * XS
ROW_DEVS = YS * CORES
MY_ROWS = ROWS // ROW_DEVS
MY_COLS = COLS // COL_DEVS
OWN = MY_ROWS // COL_DEVS
GROUP = OWN * XS
GROUPS = MY_ROWS // GROUP
HALF = RANK // 2
SHARE = HALF // CORES
PART = SHARE // 2
PIECE = OWN // 2
SPAN = GROUP // 2
UNITS = ((0, 0, 896), (0, 896, 768), (1, 0, 512), (1, 512, 512), (1, 1024, 640))
LATE = (2, 3, 4)
PIVOTS = 16

CORE, FIRST_A, FIRST_B, SECOND_A, SECOND_B, PAIR = range(6)
KINDS = 6

FAR_FIRST = ((2, 2), (2, 1), (2, 3), (1, 2), (3, 2), (1, 1), (3, 3), (1, 3), (3, 1), (2, 0), (0, 2), (1, 0), (3, 0), (0, 1), (0, 3))


def dot(a, b, precision=None):
    return jnp.dot(a, b, precision=precision, preferred_element_type=F32)


def split(a):
    high = a.astype(BF16)
    return high, (a - high.astype(F32)).astype(BF16)


def dot3(a, b):
    ah, al = split(a)
    bh, bl = split(b)
    return dot(ah, bh) + (dot(ah, bl) + dot(al, bh))


def iota(shape, dim):
    return lax.broadcasted_iota(jnp.int32, shape, dim)


def eliminate(rows, first):
    ri, ci = iota(rows.shape, 0), iota(rows.shape, 1)
    cols = [jnp.broadcast_to(rows[:, first + j : first + j + 1], rows.shape) for j in range(PIVOTS)]
    for k in range(PIVOTS):
        scale = lax.rsqrt(cols[k][k : k + 1, :])
        row = jnp.where(ci[:1] == first + k, scale, rows[k : k + 1, :] * scale)
        mult = jnp.where(ri > k, cols[k] * scale, 0.0)
        cleared = jnp.where((ci == first + k) & (ri > k), 0.0, rows)
        rows = jnp.where(ri == k, row, cleared - mult * row)
        for j in range(k + 1, PIVOTS):
            cols[j] = cols[j] - mult * (cols[j][k : k + 1, :] * scale)
    return jnp.where((ci > ri + first) & (ci < first + PIVOTS), 0.0, rows)


def cholesky_block(work, block):
    first = block * PIVOTS
    after = first + PIVOTS
    done = eliminate(work[first:after, :], first)
    work[first:after, :] = done
    if after < RANK:
        ci = iota(done.shape, 1)
        factor = jnp.where(ci >= after, done, 0.0).T
        rest = work[after:, :]
        cj = iota(rest.shape, 1)
        rest = jnp.where((cj >= first) & (cj < after), 0.0, rest)
        work[after:, :] = rest - dot(factor[after:, :], done, HI)


def main_kernel(
    mom, grad, rf, w,
    nm, wv, ortho, rt, rcut, sq,
    hi, lo, gbuf, rbuf, rcat, psend, prs, pan, pan_t, pt, gram_part, gram_pair, gram_in, gram, sloc, cbuf, y1, in1, y2, in2, stf, sq_send, sq_in,
    load_sem, mom_sem, grad_sem,
    rs_send, rs_recv, ag_send, ag_recv, g_send, g_recv, y_send, y_recv, q_send, q_recv,
):
    row = lax.axis_index("row")
    col = lax.axis_index("col")
    y, core = row // CORES, row % CORES
    z, x = col // XS, col % XS
    pair = (y * CORES + 1 - core, col)
    near = ((y + 1 - 2 * (y % 2)) * CORES + core, col)
    far = ((YS - 1 - y) * CORES + core, col)

    rf_copy = pltpu.make_async_copy(rf, rbuf, load_sem.at[0])
    rf_copy.start()
    g0 = (x + z) % GROUPS

    def group_of(j):
        return (g0 + 1 + j) % GROUPS

    def other(step):
        return (z + step[0]) % ZS * XS + (x + step[1]) % XS

    def load(j):
        rows = pl.ds(pl.multiple_of(group_of(j) * GROUP, GROUP), GROUP)
        return (
            pltpu.make_async_copy(mom.at[rows, :], nm.at[rows, :], mom_sem.at[j]),
            pltpu.make_async_copy(grad.at[rows, :], gbuf.at[rows, :], grad_sem.at[j]),
        )

    for c in load(0):
        c.start()

    barrier = pltpu.get_barrier_semaphore()

    def greet_col(k, _):
        pl.semaphore_signal(barrier, inc=1, device_id=(row, (col + k) % COL_DEVS), device_id_type=MESH)
        return 0

    lax.fori_loop(1, COL_DEVS, greet_col, 0)
    row_peers = [pair] + [(((y + k) % YS) * CORES + core, col) for k in (2, 1, 3)]
    for peer in row_peers:
        pl.semaphore_signal(barrier, inc=1, device_id=peer, device_id_type=MESH)

    for j in range(1, GROUPS):
        for c in load(j):
            c.start()

    rf_copy.wait()
    rh, rl = split(rbuf[...])
    rcat[:, :RANK] = rh
    rcat[:, RANK:] = rl

    def place(c):
        cz, cx = c // XS, c % XS
        return (cx + cz) % GROUPS * XS + cx

    def own_rows(c):
        return pl.ds(pl.multiple_of(place(c) * OWN, OWN), OWN)

    def rs_copy(to, slot):
        return pltpu.make_async_remote_copy(
            src_ref=psend.at[own_rows(to), :], dst_ref=prs.at[slot], send_sem=rs_send.at[to], recv_sem=rs_recv.at[slot],
            device_id=(row, to), device_id_type=MESH)

    def panel_group(j, _):
        for c in load(j):
            c.wait()
        g = group_of(j)
        rows = pl.ds(pl.multiple_of(g * GROUP, GROUP), GROUP)
        a = nm[rows, :] + gbuf[rows, :].astype(F32)
        nm[rows, :] = a
        ah, al = split(a)
        hi[rows, :] = ah
        lo[rows, :] = al
        p = dot(ah, rcat[...])
        p = p[:, :RANK] + p[:, RANK:] + dot(al, rcat[:, :RANK])
        for t in range(XS):
            at = pl.multiple_of(g * GROUP + t * OWN, OWN)
            psend[pl.ds(at, PIECE), :] = p[t * PIECE : (t + 1) * PIECE]
            psend[pl.ds(at + PIECE, PIECE), :] = p[SPAN + t * PIECE : SPAN + (t + 1) * PIECE]

        @pl.when(j == 0)
        def _():
            pl.semaphore_wait(barrier, COL_DEVS - 1 + len(row_peers))

        for t in range(XS):
            to = ((g + GROUPS - t) % GROUPS) * XS + t

            @pl.when(to != col)
            def _():
                rs_copy(to, col).start()

        return 0

    lax.fori_loop(0, GROUPS, panel_group, 0)
    w_copy = pltpu.make_async_copy(w, wv, load_sem.at[1])
    w_copy.start()

    mine = own_rows(col)

    total = psend[mine, :]
    for step in reversed(FAR_FIRST):
        src = other(step)
        rs_copy(src, src).wait_recv()
        total = total + prs[src]

    def own_block(c):
        return pl.ds(pl.multiple_of(place(c) * PIECE, PIECE), PIECE)

    for h in range(2):
        half = total[:, h * HALF : (h + 1) * HALF]
        pan[h, own_block(col), :] = jnp.concatenate([half[:PIECE], half[PIECE:]], axis=1)

    def ag_copy(h, to, owner):
        block = pan.at[h, own_block(owner), :]
        return pltpu.make_async_remote_copy(
            src_ref=block, dst_ref=block, send_sem=ag_send.at[h, to], recv_sem=ag_recv.at[h, owner],
            device_id=(row, to), device_id_type=MESH)

    for h in range(2):
        for step in FAR_FIRST:
            ag_copy(h, other(step), col).start()

    def arrive(h):
        for step in reversed(FAR_FIRST):
            src = other(step)
            ag_copy(h, src, src).wait_recv()
        block = pan[h].T
        for g in range(GROUPS):
            for i in range(2):
                at = pl.ds(g * GROUP + i * SPAN, SPAN)
                piece = block[i * HALF : (i + 1) * HALF, g * SPAN : (g + 1) * SPAN]
                high, low = split(piece)
                pan_t[h * HALF : (h + 1) * HALF, at] = piece
                pt[h, :HALF, at] = high
                pt[h, HALF:, at] = low

    arrive(0)

    ours = pl.ds(pl.multiple_of(core * HALF, HALF), HALF)
    theirs = pl.ds(pl.multiple_of((1 - core) * HALF, HALF), HALF)

    def gram_copy(kind, src, dst, to):
        return pltpu.make_async_remote_copy(
            src_ref=src, dst_ref=dst, send_sem=g_send.at[kind], recv_sem=g_recv.at[kind], device_id=to, device_id_type=MESH)

    gram_scatter = gram_copy(0, gram_part.at[theirs, :], gram_pair, pair)
    gram_gather = gram_copy(1, gram.at[ours, :], gram.at[ours, :], pair)

    def gram_y(to, slot):
        return pltpu.make_async_remote_copy(
            src_ref=gram_in.at[slot], dst_ref=gram_in.at[slot], send_sem=g_send.at[2 + to], recv_sem=g_recv.at[2 + slot],
            device_id=(to * CORES + core, col), device_id_type=MESH)

    def gram_1():
        gram_scatter.wait_recv()
        gram_in[y] = gram_part[ours, :] + gram_pair[...]
        for k in (2, 1, 3):
            gram_y((y + k) % YS, y).start()

    def gram_2():
        for k in (1, 3, 2):
            src = (y + k) % YS
            gram_y(src, src).wait_recv()
        gram[ours, :] = (gram_in[0] + gram_in[1]) + (gram_in[2] + gram_in[3])
        gram_gather.start()

    def ycopy(kind, c, src, dst, to):
        return pltpu.make_async_remote_copy(
            src_ref=src, dst_ref=dst, send_sem=y_send.at[c, kind], recv_sem=y_recv.at[c, kind], device_id=to, device_id_type=MESH)

    def lanes(u):
        return pl.ds(*UNITS[u][1:])

    def core_copy(u):
        return ycopy(CORE, u, sloc.at[ranks_of(u, 1 - core), lanes(u)], cbuf.at[share(u), lanes(u)], pair)

    def ranks_of(u, c):
        return pl.ds(pl.multiple_of(UNITS[u][0] * HALF + c * SHARE, SHARE), SHARE)

    def share(u):
        return pl.ds(UNITS[u][0] * SHARE, SHARE)

    def part_rows(u, part):
        return pl.ds(UNITS[u][0] * SHARE + part * PART, PART)

    def first_copies(u):
        return (
            ycopy(FIRST_A, u, y1.at[part_rows(u, 0), lanes(u)], in1.at[part_rows(u, 0), lanes(u)], near),
            ycopy(FIRST_B, u, y1.at[part_rows(u, 1), lanes(u)], in1.at[part_rows(u, 1), lanes(u)], far),
        )

    def second_copies(u):
        return (
            ycopy(SECOND_A, u, y2.at[part_rows(u, 0), lanes(u)], in2.at[part_rows(u, 0), lanes(u)], far),
            ycopy(SECOND_B, u, y2.at[part_rows(u, 1), lanes(u)], in2.at[part_rows(u, 1), lanes(u)], near),
        )

    def pair_copy(u):
        block = stf.at[ranks_of(u, core), lanes(u)]
        return ycopy(PAIR, u, block, block, pair)

    def product(u):
        h = UNITS[u][0]
        t = dot(pt[h], hi[:, lanes(u)])
        sloc[pl.ds(h * HALF, HALF), lanes(u)] = t[:HALF] + t[HALF:] + dot(pt[h, :HALF, :], lo[:, lanes(u)])
        core_copy(u).start()

    def first(u):
        core_copy(u).wait_recv()
        y1[share(u), lanes(u)] = sloc[ranks_of(u, core), lanes(u)] + cbuf[share(u), lanes(u)]
        for cp in first_copies(u):
            cp.start()

    def second(u):
        for part, cp in enumerate(first_copies(u)):
            cp.wait_recv()
            at = part_rows(u, part)
            y2[at, lanes(u)] = y1[at, lanes(u)] + in1[at, lanes(u)]
            second_copies(u)[part].start()

    def third(u):
        for cp in second_copies(u):
            cp.wait_recv()
        stf[ranks_of(u, core), lanes(u)] = y2[share(u), lanes(u)] + in2[share(u), lanes(u)]
        pair_copy(u).start()

    product(0)
    product(1)
    first(0)
    first(1)
    arrive(1)
    both = jnp.concatenate([pt[0, :HALF, :], pt[1, :HALF, :], pt[0, HALF:, :], pt[1, HALF:, :]], axis=0)
    t = lax.dot_general(both, both, (((1,), (1,)), ((), ())), preferred_element_type=F32)
    gram_part[...] = t[:RANK, :RANK] + (t[:RANK, RANK:] + t[RANK:, :RANK] + t[RANK:, RANK:])
    gram_scatter.start()
    product(2)
    product(3)
    product(4)
    gram_1()
    first(2)
    first(3)
    first(4)
    second(0)
    second(1)
    second(2)

    gram_2()
    second(3)
    second(4)
    gram_scatter.wait_send()
    gram_gather.wait()
    steps = {2: (third, 0), 3: (third, 1), 4: (third, 2), 5: (third, 3), 6: (third, 4)}
    for b in range(RANK // PIVOTS):
        cholesky_block(gram, b)
        if b in steps:
            move, u = steps[b]
            move(u)
    inverse = jnp.where(iota((RANK, RANK), 0) >= iota((RANK, RANK), 1), gram[...], 0.0)

    inverse_cut = jnp.concatenate(split(inverse), axis=0)
    squares = jnp.zeros((RANK, RANK), F32)
    for u in range(LATE[0]):
        pair_copy(u).wait_recv()
    for u in LATE:
        pair_copy(u).wait_recv()
        high, low = split(stf[:, lanes(u)])
        t = dot(inverse_cut, high)
        part = t[:RANK] + (t[RANK:] + dot(inverse_cut[:RANK], low))
        rt[:, lanes(u)] = part
        for i in range(UNITS[u][2] // RANK):
            tile = part[:, i * RANK : (i + 1) * RANK]
            squares += tile * tile
    sq_send[...] = jnp.broadcast_to(jnp.sum(squares.T, axis=0, keepdims=True), sq_send.shape)

    def q_copy(to, slot):
        return pltpu.make_async_remote_copy(
            src_ref=sq_send, dst_ref=sq_in.at[slot], send_sem=q_send.at[to], recv_sem=q_recv.at[slot],
            device_id=(row, to), device_id_type=MESH)

    for step in FAR_FIRST:
        q_copy(other(step), col).start()

    ortho[...] = dot3(inverse, pan_t[...]).T
    high, low = split(rt[...])
    rcut[:RANK, :] = high
    rcut[RANK : 2 * RANK, :] = high
    rcut[2 * RANK :, :] = low

    def momentum(i, _):
        rows = pl.ds(pl.multiple_of(i * GROUP, GROUP), GROUP)
        nm[rows, :] = nm[rows, :] - 0.2 * dot(ortho[rows, :].astype(BF16), rcut[:RANK, :])
        return 0

    lax.fori_loop(0, GROUPS, momentum, 0)

    w_copy.wait()

    def sent(k, _):
        to = (col + k) % COL_DEVS
        rs_copy(to, col).wait_send()
        ag_copy(0, to, col).wait_send()
        ag_copy(1, to, col).wait_send()
        return 0

    lax.fori_loop(1, COL_DEVS, sent, 0)
    for k in (1, 2, 3):
        gram_y((y + k) % YS, y).wait_send()
    for u in range(len(UNITS)):
        for cp in (core_copy(u), pair_copy(u)) + first_copies(u) + second_copies(u):
            cp.wait_send()

    total = sq_send[...]
    for step in reversed(FAR_FIRST):
        src = other(step)
        q_copy(src, src).wait_recv()
        total = total + sq_in[src]
    sq[...] = total

    def q_sent(k, _):
        q_copy((col + k) % COL_DEVS, col).wait_send()
        return 0

    lax.fori_loop(1, COL_DEVS, q_sent, 0)


def final_kernel(nm, wv, ortho, rt, rcut, sq, new_w, new_m, new_r, out, r_out, m_sem, w_sem, r_sem):
    m_copy = pltpu.make_async_copy(nm, new_m, m_sem)
    m_copy.start()
    scale = jnp.sqrt(F32(COLS)) / jnp.sqrt(sq[:1, :] + 1e-06)
    factor = 0.5 * jnp.sqrt(F32(ROWS) / F32(RANK))

    def w_copy(i):
        rows = pl.ds(pl.multiple_of(i * GROUP, GROUP), GROUP)
        return pltpu.make_async_copy(out.at[rows, :], new_w.at[rows, :], w_sem.at[i])

    def weight(i, _):
        rows = pl.ds(pl.multiple_of(i * GROUP, GROUP), GROUP)
        high, low = split(ortho[rows, :] * (scale * factor))
        step = dot(jnp.concatenate([high, low], axis=1), rcut[: 2 * RANK, :]) + dot(high, rcut[2 * RANK :, :])
        out[rows, :] = (wv[rows, :].astype(F32) - step).astype(BF16)
        w_copy(i).start()
        return 0

    lax.fori_loop(0, GROUPS, weight, 0)
    r_out[...] = rt[...].T * scale
    r_copy = pltpu.make_async_copy(r_out, new_r, r_sem)
    r_copy.start()

    def done(i, _):
        w_copy(i).wait()
        return 0

    lax.fori_loop(0, GROUPS, done, 0)
    m_copy.wait()
    r_copy.wait()


def shards(weight, momentum, gradient, right_factor):
    hbm = pl.BlockSpec(memory_space=pltpu.HBM)
    vmem = pl.BlockSpec(memory_space=pltpu.VMEM)
    dma = pltpu.SemaphoreType.DMA
    held = pl.pallas_call(
        main_kernel,
        out_shape=(
            pltpu.VMEM((MY_ROWS, MY_COLS), F32),
            pltpu.VMEM((MY_ROWS, MY_COLS), BF16),
            pltpu.VMEM((MY_ROWS, RANK), F32),
            pltpu.VMEM((RANK, MY_COLS), F32),
            pltpu.VMEM((3 * RANK, MY_COLS), BF16),
            pltpu.VMEM((8, RANK), F32),
        ),
        in_specs=[hbm] * 4,
        out_specs=(vmem,) * 6,
        scratch_shapes=[
            pltpu.VMEM((MY_ROWS, MY_COLS), BF16),
            pltpu.VMEM((MY_ROWS, MY_COLS), BF16),
            pltpu.VMEM((MY_ROWS, MY_COLS), BF16),
            pltpu.VMEM((MY_COLS, RANK), F32),
            pltpu.VMEM((MY_COLS, 2 * RANK), BF16),
            pltpu.VMEM((MY_ROWS, RANK), F32),
            pltpu.VMEM((COL_DEVS, OWN, RANK), F32),
            pltpu.VMEM((2, MY_ROWS // 2, RANK), F32),
            pltpu.VMEM((RANK, MY_ROWS), F32),
            pltpu.VMEM((2, RANK, MY_ROWS), BF16),
            pltpu.VMEM((RANK, RANK), F32),
            pltpu.VMEM((HALF, RANK), F32),
            pltpu.VMEM((YS, HALF, RANK), F32),
            pltpu.VMEM((RANK, RANK), F32),
            pltpu.VMEM((RANK, MY_COLS), F32),
            pltpu.VMEM((HALF, MY_COLS), F32),
            pltpu.VMEM((HALF, MY_COLS), F32),
            pltpu.VMEM((HALF, MY_COLS), F32),
            pltpu.VMEM((HALF, MY_COLS), F32),
            pltpu.VMEM((HALF, MY_COLS), F32),
            pltpu.VMEM((RANK, MY_COLS), F32),
            pltpu.VMEM((8, RANK), F32),
            pltpu.VMEM((COL_DEVS, 8, RANK), F32),
            dma((2,)), dma((GROUPS,)), dma((GROUPS,)),
            dma((COL_DEVS,)), dma((COL_DEVS,)), dma((2, COL_DEVS)), dma((2, COL_DEVS)),
            dma((2 + YS,)), dma((2 + YS,)),
            dma((len(UNITS), KINDS)), dma((len(UNITS), KINDS)),
            dma((COL_DEVS,)), dma((COL_DEVS,)),
        ],
        compiler_params=pltpu.CompilerParams(collective_id=0, has_side_effects=True, vmem_limit_bytes=50 << 20),
        name="dion_main",
    )(momentum, gradient, right_factor, weight)
    return pl.pallas_call(
        final_kernel,
        out_shape=(
            jax.ShapeDtypeStruct((MY_ROWS, MY_COLS), BF16),
            jax.ShapeDtypeStruct((MY_ROWS, MY_COLS), F32),
            jax.ShapeDtypeStruct((MY_COLS, RANK), F32),
        ),
        in_specs=[vmem] * 6,
        out_specs=(hbm,) * 3,
        scratch_shapes=[
            pltpu.VMEM((MY_ROWS, MY_COLS), BF16),
            pltpu.VMEM((MY_COLS, RANK), F32),
            dma, dma((GROUPS,)), dma,
        ],
        compiler_params=pltpu.CompilerParams(vmem_limit_bytes=24 << 20),
        name="dion_final",
    )(*held)


def solution(mesh):
    placed = (P("row", "col"), P("row", "col"), P("row", "col"), P("col", None))
    return jax.shard_map(
        shards,
        mesh=mesh,
        in_specs=placed,
        out_specs=(P("row", "col"), P("row", "col"), P("col", None)),
        check_vma=False,
    )
```

```python
import jax
import jax.numpy as jnp
from jax import lax
from jax.experimental import pallas as pl
from jax.experimental.pallas import tpu as pltpu
from jax.sharding import PartitionSpec as P

ROWS = 8192
COLS = 26624
RANK = 128
HI = lax.Precision.HIGHEST
MESH = pl.DeviceIdType.MESH
F32 = jnp.float32
BF16 = jnp.bfloat16

ZS, XS, YS, CORES = 4, 4, 4, 2
COL_DEVS = ZS * XS
ROW_DEVS = YS * CORES
MY_ROWS = ROWS // ROW_DEVS
MY_COLS = COLS // COL_DEVS
OWN = MY_ROWS // COL_DEVS
GROUP = OWN * XS
GROUPS = MY_ROWS // GROUP
HALF = RANK // 2
SHARE = HALF // CORES
PART = SHARE // 2
PIECE = OWN // 2
SPAN = GROUP // 2
UNITS = ((0, 0, 896), (0, 896, 768), (1, 0, 512), (1, 512, 512), (1, 1024, 640))
LATE = (2, 3, 4)
PIVOTS = 16

CORE, FIRST_A, FIRST_B, SECOND_A, SECOND_B, PAIR = range(6)
KINDS = 6

FAR_FIRST = ((2, 2), (2, 1), (2, 3), (1, 2), (3, 2), (1, 1), (3, 3), (1, 3), (3, 1), (2, 0), (0, 2), (1, 0), (3, 0), (0, 1), (0, 3))


def dot(a, b, precision=None):
    return jnp.dot(a, b, precision=precision, preferred_element_type=F32)


def split(a):
    high = a.astype(BF16)
    return high, (a - high.astype(F32)).astype(BF16)


def dot3(a, b):
    ah, al = split(a)
    bh, bl = split(b)
    return dot(ah, bh) + (dot(ah, bl) + dot(al, bh))


def iota(shape, dim):
    return lax.broadcasted_iota(jnp.int32, shape, dim)


def eliminate(rows, first):
    ri, ci = iota(rows.shape, 0), iota(rows.shape, 1)
    cols = [jnp.broadcast_to(rows[:, first + j : first + j + 1], rows.shape) for j in range(PIVOTS)]
    for k in range(PIVOTS):
        scale = lax.rsqrt(cols[k][k : k + 1, :])
        row = jnp.where(ci[:1] == first + k, scale, rows[k : k + 1, :] * scale)
        mult = jnp.where(ri > k, cols[k] * scale, 0.0)
        cleared = jnp.where((ci == first + k) & (ri > k), 0.0, rows)
        rows = jnp.where(ri == k, row, cleared - mult * row)
        for j in range(k + 1, PIVOTS):
            cols[j] = cols[j] - mult * (cols[j][k : k + 1, :] * scale)
    return jnp.where((ci > ri + first) & (ci < first + PIVOTS), 0.0, rows)


def cholesky_block(work, block):
    first = block * PIVOTS
    after = first + PIVOTS
    done = eliminate(work[first:after, :], first)
    work[first:after, :] = done
    if after < RANK:
        ci = iota(done.shape, 1)
        factor = jnp.where(ci >= after, done, 0.0).T
        rest = work[after:, :]
        cj = iota(rest.shape, 1)
        rest = jnp.where((cj >= first) & (cj < after), 0.0, rest)
        work[after:, :] = rest - dot(factor[after:, :], done, HI)


def main_kernel(
    mom, grad, rf, w,
    nm, wv, ortho, rt, rcut, sq,
    hi, lo, gbuf, rbuf, rcat, psend, prs, pan, pan_t, pt, gram_part, gram_pair, gram_in, gram, sloc, cbuf, y1, in1, y2, in2, stf, sq_send, sq_in,
    load_sem, mom_sem, grad_sem,
    rs_send, rs_recv, ag_send, ag_recv, g_send, g_recv, y_send, y_recv, q_send, q_recv,
):
    row = lax.axis_index("row")
    col = lax.axis_index("col")
    y, core = row // CORES, row % CORES
    z, x = col // XS, col % XS
    pair = (y * CORES + 1 - core, col)
    near = ((y + 1 - 2 * (y % 2)) * CORES + core, col)
    far = ((YS - 1 - y) * CORES + core, col)

    rf_copy = pltpu.make_async_copy(rf, rbuf, load_sem.at[0])
    rf_copy.start()
    g0 = (x + z) % GROUPS

    def group_of(j):
        return (g0 + 1 + j) % GROUPS

    def other(step):
        return (z + step[0]) % ZS * XS + (x + step[1]) % XS

    def load(j):
        rows = pl.ds(pl.multiple_of(group_of(j) * GROUP, GROUP), GROUP)
        return (
            pltpu.make_async_copy(mom.at[rows, :], nm.at[rows, :], mom_sem.at[j]),
            pltpu.make_async_copy(grad.at[rows, :], gbuf.at[rows, :], grad_sem.at[j]),
        )

    for c in load(0):
        c.start()

    barrier = pltpu.get_barrier_semaphore()

    def greet_col(k, _):
        pl.semaphore_signal(barrier, inc=1, device_id=(row, (col + k) % COL_DEVS), device_id_type=MESH)
        return 0

    lax.fori_loop(1, COL_DEVS, greet_col, 0)
    row_peers = [pair] + [(((y + k) % YS) * CORES + core, col) for k in (2, 1, 3)]
    for peer in row_peers:
        pl.semaphore_signal(barrier, inc=1, device_id=peer, device_id_type=MESH)

    for j in range(1, GROUPS):
        for c in load(j):
            c.start()

    rf_copy.wait()
    rh, rl = split(rbuf[...])
    rcat[:, :RANK] = rh
    rcat[:, RANK:] = rl

    def place(c):
        cz, cx = c // XS, c % XS
        return (cx + cz) % GROUPS * XS + cx

    def own_rows(c):
        return pl.ds(pl.multiple_of(place(c) * OWN, OWN), OWN)

    def rs_copy(to, slot):
        return pltpu.make_async_remote_copy(
            src_ref=psend.at[own_rows(to), :], dst_ref=prs.at[slot], send_sem=rs_send.at[to], recv_sem=rs_recv.at[slot],
            device_id=(row, to), device_id_type=MESH)

    def panel_group(j, _):
        for c in load(j):
            c.wait()
        g = group_of(j)
        rows = pl.ds(pl.multiple_of(g * GROUP, GROUP), GROUP)
        a = nm[rows, :] + gbuf[rows, :].astype(F32)
        nm[rows, :] = a
        ah, al = split(a)
        hi[rows, :] = ah
        lo[rows, :] = al
        p = dot(ah, rcat[...])
        p = p[:, :RANK] + p[:, RANK:] + dot(al, rcat[:, :RANK])
        for t in range(XS):
            at = pl.multiple_of(g * GROUP + t * OWN, OWN)
            psend[pl.ds(at, PIECE), :] = p[t * PIECE : (t + 1) * PIECE]
            psend[pl.ds(at + PIECE, PIECE), :] = p[SPAN + t * PIECE : SPAN + (t + 1) * PIECE]

        @pl.when(j == 0)
        def _():
            pl.semaphore_wait(barrier, COL_DEVS - 1 + len(row_peers))

        for t in range(XS):
            to = ((g + GROUPS - t) % GROUPS) * XS + t

            @pl.when(to != col)
            def _():
                rs_copy(to, col).start()

        return 0

    lax.fori_loop(0, GROUPS, panel_group, 0)
    w_copy = pltpu.make_async_copy(w, wv, load_sem.at[1])
    w_copy.start()

    mine = own_rows(col)

    total = psend[mine, :]
    for step in reversed(FAR_FIRST):
        src = other(step)
        rs_copy(src, src).wait_recv()
        total = total + prs[src]

    def own_block(c):
        return pl.ds(pl.multiple_of(place(c) * PIECE, PIECE), PIECE)

    def ag_copy(h, to, owner):
        block = pan.at[h, own_block(owner), :]
        return pltpu.make_async_remote_copy(
            src_ref=block, dst_ref=block, send_sem=ag_send.at[h, to], recv_sem=ag_recv.at[h, owner],
            device_id=(row, to), device_id_type=MESH)

    for h in range(2):
        half = total[:, h * HALF : (h + 1) * HALF]
        pan[h, own_block(col), :] = jnp.concatenate([half[:PIECE], half[PIECE:]], axis=1)
        for step in FAR_FIRST:
            ag_copy(h, other(step), col).start()

    def arrive(h):
        for step in reversed(FAR_FIRST):
            src = other(step)
            ag_copy(h, src, src).wait_recv()
        block = pan[h].T
        for g in range(GROUPS):
            for i in range(2):
                at = pl.ds(g * GROUP + i * SPAN, SPAN)
                piece = block[i * HALF : (i + 1) * HALF, g * SPAN : (g + 1) * SPAN]
                high, low = split(piece)
                pan_t[h * HALF : (h + 1) * HALF, at] = piece
                pt[h, :HALF, at] = high
                pt[h, HALF:, at] = low

    arrive(0)

    ours = pl.ds(pl.multiple_of(core * HALF, HALF), HALF)
    theirs = pl.ds(pl.multiple_of((1 - core) * HALF, HALF), HALF)

    def gram_copy(kind, src, dst, to):
        return pltpu.make_async_remote_copy(
            src_ref=src, dst_ref=dst, send_sem=g_send.at[kind], recv_sem=g_recv.at[kind], device_id=to, device_id_type=MESH)

    gram_scatter = gram_copy(0, gram_part.at[theirs, :], gram_pair, pair)
    gram_gather = gram_copy(1, gram.at[ours, :], gram.at[ours, :], pair)

    def gram_y(to, slot):
        return pltpu.make_async_remote_copy(
            src_ref=gram_in.at[slot], dst_ref=gram_in.at[slot], send_sem=g_send.at[2 + to], recv_sem=g_recv.at[2 + slot],
            device_id=(to * CORES + core, col), device_id_type=MESH)

    def gram_1():
        gram_scatter.wait_recv()
        gram_in[y] = gram_part[ours, :] + gram_pair[...]
        for k in (2, 1, 3):
            gram_y((y + k) % YS, y).start()

    def gram_2():
        for k in (1, 3, 2):
            src = (y + k) % YS
            gram_y(src, src).wait_recv()
        gram[ours, :] = (gram_in[0] + gram_in[1]) + (gram_in[2] + gram_in[3])
        gram_gather.start()

    def ycopy(kind, c, src, dst, to):
        return pltpu.make_async_remote_copy(
            src_ref=src, dst_ref=dst, send_sem=y_send.at[c, kind], recv_sem=y_recv.at[c, kind], device_id=to, device_id_type=MESH)

    def lanes(u):
        return pl.ds(*UNITS[u][1:])

    def core_copy(u):
        return ycopy(CORE, u, sloc.at[ranks_of(u, 1 - core), lanes(u)], cbuf.at[share(u), lanes(u)], pair)

    def ranks_of(u, c):
        return pl.ds(pl.multiple_of(UNITS[u][0] * HALF + c * SHARE, SHARE), SHARE)

    def share(u):
        return pl.ds(UNITS[u][0] * SHARE, SHARE)

    def part_rows(u, part):
        return pl.ds(UNITS[u][0] * SHARE + part * PART, PART)

    def first_copies(u):
        return (
            ycopy(FIRST_A, u, y1.at[part_rows(u, 0), lanes(u)], in1.at[part_rows(u, 0), lanes(u)], near),
            ycopy(FIRST_B, u, y1.at[part_rows(u, 1), lanes(u)], in1.at[part_rows(u, 1), lanes(u)], far),
        )

    def second_copies(u):
        return (
            ycopy(SECOND_A, u, y2.at[part_rows(u, 0), lanes(u)], in2.at[part_rows(u, 0), lanes(u)], far),
            ycopy(SECOND_B, u, y2.at[part_rows(u, 1), lanes(u)], in2.at[part_rows(u, 1), lanes(u)], near),
        )

    def pair_copy(u):
        block = stf.at[ranks_of(u, core), lanes(u)]
        return ycopy(PAIR, u, block, block, pair)

    def product(u):
        h = UNITS[u][0]
        t = dot(pt[h], hi[:, lanes(u)])
        sloc[pl.ds(h * HALF, HALF), lanes(u)] = t[:HALF] + t[HALF:] + dot(pt[h, :HALF, :], lo[:, lanes(u)])
        core_copy(u).start()

    def first(u):
        core_copy(u).wait_recv()
        y1[share(u), lanes(u)] = sloc[ranks_of(u, core), lanes(u)] + cbuf[share(u), lanes(u)]
        for cp in first_copies(u):
            cp.start()

    def second(u):
        for part, cp in enumerate(first_copies(u)):
            cp.wait_recv()
            at = part_rows(u, part)
            y2[at, lanes(u)] = y1[at, lanes(u)] + in1[at, lanes(u)]
            second_copies(u)[part].start()

    def third(u):
        for cp in second_copies(u):
            cp.wait_recv()
        stf[ranks_of(u, core), lanes(u)] = y2[share(u), lanes(u)] + in2[share(u), lanes(u)]
        pair_copy(u).start()

    product(0)
    product(1)
    first(0)
    first(1)
    arrive(1)
    both = jnp.concatenate([pt[0, :HALF, :], pt[1, :HALF, :], pt[0, HALF:, :], pt[1, HALF:, :]], axis=0)
    t = lax.dot_general(both, both, (((1,), (1,)), ((), ())), preferred_element_type=F32)
    gram_part[...] = t[:RANK, :RANK] + (t[:RANK, RANK:] + t[RANK:, :RANK] + t[RANK:, RANK:])
    gram_scatter.start()
    product(2)
    product(3)
    product(4)
    gram_1()
    first(2)
    first(3)
    first(4)
    second(0)
    second(1)
    second(2)

    gram_2()
    second(3)
    second(4)
    gram_scatter.wait_send()
    gram_gather.wait()
    steps = {2: (third, 0), 3: (third, 1), 4: (third, 2), 5: (third, 3), 6: (third, 4)}
    for b in range(RANK // PIVOTS):
        cholesky_block(gram, b)
        if b in steps:
            move, u = steps[b]
            move(u)
    inverse = jnp.where(iota((RANK, RANK), 0) >= iota((RANK, RANK), 1), gram[...], 0.0)

    inverse_cut = jnp.concatenate(split(inverse), axis=0)
    squares = jnp.zeros((RANK, RANK), F32)
    for u in range(LATE[0]):
        pair_copy(u).wait_recv()
    for u in LATE:
        pair_copy(u).wait_recv()
        high, low = split(stf[:, lanes(u)])
        t = dot(inverse_cut, high)
        part = t[:RANK] + (t[RANK:] + dot(inverse_cut[:RANK], low))
        rt[:, lanes(u)] = part
        for i in range(UNITS[u][2] // RANK):
            tile = part[:, i * RANK : (i + 1) * RANK]
            squares += tile * tile
    sq_send[...] = jnp.broadcast_to(jnp.sum(squares.T, axis=0, keepdims=True), sq_send.shape)

    def q_copy(to, slot):
        return pltpu.make_async_remote_copy(
            src_ref=sq_send, dst_ref=sq_in.at[slot], send_sem=q_send.at[to], recv_sem=q_recv.at[slot],
            device_id=(row, to), device_id_type=MESH)

    for step in FAR_FIRST:
        q_copy(other(step), col).start()

    ortho[...] = dot3(inverse, pan_t[...]).T
    high, low = split(rt[...])
    rcut[:RANK, :] = high
    rcut[RANK : 2 * RANK, :] = high
    rcut[2 * RANK :, :] = low

    def momentum(i, _):
        rows = pl.ds(pl.multiple_of(i * GROUP, GROUP), GROUP)
        nm[rows, :] = nm[rows, :] - 0.2 * dot(ortho[rows, :].astype(BF16), rcut[:RANK, :])
        return 0

    lax.fori_loop(0, GROUPS, momentum, 0)

    w_copy.wait()

    def sent(k, _):
        to = (col + k) % COL_DEVS
        rs_copy(to, col).wait_send()
        ag_copy(0, to, col).wait_send()
        ag_copy(1, to, col).wait_send()
        return 0

    lax.fori_loop(1, COL_DEVS, sent, 0)
    for k in (1, 2, 3):
        gram_y((y + k) % YS, y).wait_send()
    for u in range(len(UNITS)):
        for cp in (core_copy(u), pair_copy(u)) + first_copies(u) + second_copies(u):
            cp.wait_send()

    total = sq_send[...]
    for step in reversed(FAR_FIRST):
        src = other(step)
        q_copy(src, src).wait_recv()
        total = total + sq_in[src]
    sq[...] = total

    def q_sent(k, _):
        q_copy((col + k) % COL_DEVS, col).wait_send()
        return 0

    lax.fori_loop(1, COL_DEVS, q_sent, 0)


def final_kernel(nm, wv, ortho, rt, rcut, sq, new_w, new_m, new_r, out, r_out, m_sem, w_sem, r_sem):
    m_copy = pltpu.make_async_copy(nm, new_m, m_sem)
    m_copy.start()
    scale = jnp.sqrt(F32(COLS)) / jnp.sqrt(sq[:1, :] + 1e-06)
    factor = 0.5 * jnp.sqrt(F32(ROWS) / F32(RANK))

    def w_copy(i):
        rows = pl.ds(pl.multiple_of(i * GROUP, GROUP), GROUP)
        return pltpu.make_async_copy(out.at[rows, :], new_w.at[rows, :], w_sem.at[i])

    def weight(i, _):
        rows = pl.ds(pl.multiple_of(i * GROUP, GROUP), GROUP)
        high, low = split(ortho[rows, :] * (scale * factor))
        step = dot(jnp.concatenate([high, low], axis=1), rcut[: 2 * RANK, :]) + dot(high, rcut[2 * RANK :, :])
        out[rows, :] = (wv[rows, :].astype(F32) - step).astype(BF16)
        w_copy(i).start()
        return 0

    lax.fori_loop(0, GROUPS, weight, 0)
    r_out[...] = rt[...].T * scale
    r_copy = pltpu.make_async_copy(r_out, new_r, r_sem)
    r_copy.start()

    def done(i, _):
        w_copy(i).wait()
        return 0

    lax.fori_loop(0, GROUPS, done, 0)
    m_copy.wait()
    r_copy.wait()


def shards(weight, momentum, gradient, right_factor):
    hbm = pl.BlockSpec(memory_space=pltpu.HBM)
    vmem = pl.BlockSpec(memory_space=pltpu.VMEM)
    dma = pltpu.SemaphoreType.DMA
    held = pl.pallas_call(
        main_kernel,
        out_shape=(
            pltpu.VMEM((MY_ROWS, MY_COLS), F32),
            pltpu.VMEM((MY_ROWS, MY_COLS), BF16),
            pltpu.VMEM((MY_ROWS, RANK), F32),
            pltpu.VMEM((RANK, MY_COLS), F32),
            pltpu.VMEM((3 * RANK, MY_COLS), BF16),
            pltpu.VMEM((8, RANK), F32),
        ),
        in_specs=[hbm] * 4,
        out_specs=(vmem,) * 6,
        scratch_shapes=[
            pltpu.VMEM((MY_ROWS, MY_COLS), BF16),
            pltpu.VMEM((MY_ROWS, MY_COLS), BF16),
            pltpu.VMEM((MY_ROWS, MY_COLS), BF16),
            pltpu.VMEM((MY_COLS, RANK), F32),
            pltpu.VMEM((MY_COLS, 2 * RANK), BF16),
            pltpu.VMEM((MY_ROWS, RANK), F32),
            pltpu.VMEM((COL_DEVS, OWN, RANK), F32),
            pltpu.VMEM((2, MY_ROWS // 2, RANK), F32),
            pltpu.VMEM((RANK, MY_ROWS), F32),
            pltpu.VMEM((2, RANK, MY_ROWS), BF16),
            pltpu.VMEM((RANK, RANK), F32),
            pltpu.VMEM((HALF, RANK), F32),
            pltpu.VMEM((YS, HALF, RANK), F32),
            pltpu.VMEM((RANK, RANK), F32),
            pltpu.VMEM((RANK, MY_COLS), F32),
            pltpu.VMEM((HALF, MY_COLS), F32),
            pltpu.VMEM((HALF, MY_COLS), F32),
            pltpu.VMEM((HALF, MY_COLS), F32),
            pltpu.VMEM((HALF, MY_COLS), F32),
            pltpu.VMEM((HALF, MY_COLS), F32),
            pltpu.VMEM((RANK, MY_COLS), F32),
            pltpu.VMEM((8, RANK), F32),
            pltpu.VMEM((COL_DEVS, 8, RANK), F32),
            dma((2,)), dma((GROUPS,)), dma((GROUPS,)),
            dma((COL_DEVS,)), dma((COL_DEVS,)), dma((2, COL_DEVS)), dma((2, COL_DEVS)),
            dma((2 + YS,)), dma((2 + YS,)),
            dma((len(UNITS), KINDS)), dma((len(UNITS), KINDS)),
            dma((COL_DEVS,)), dma((COL_DEVS,)),
        ],
        compiler_params=pltpu.CompilerParams(collective_id=0, has_side_effects=True, vmem_limit_bytes=50 << 20),
        name="dion_main",
    )(momentum, gradient, right_factor, weight)
    return pl.pallas_call(
        final_kernel,
        out_shape=(
            jax.ShapeDtypeStruct((MY_ROWS, MY_COLS), BF16),
            jax.ShapeDtypeStruct((MY_ROWS, MY_COLS), F32),
            jax.ShapeDtypeStruct((MY_COLS, RANK), F32),
        ),
        in_specs=[vmem] * 6,
        out_specs=(hbm,) * 3,
        scratch_shapes=[
            pltpu.VMEM((MY_ROWS, MY_COLS), BF16),
            pltpu.VMEM((MY_COLS, RANK), F32),
            dma, dma((GROUPS,)), dma,
        ],
        compiler_params=pltpu.CompilerParams(vmem_limit_bytes=24 << 20),
        name="dion_final",
    )(*held)


def solution(mesh):
    placed = (P("row", "col"), P("row", "col"), P("row", "col"), P("col", None))
    return jax.shard_map(
        shards,
        mesh=mesh,
        in_specs=placed,
        out_specs=(P("row", "col"), P("row", "col"), P("col", None)),
        check_vma=False,
    )
```
